256 devices in a mesh: cache: 32 (over y, x, core), tp: 8 (over z).
Axes of the slice: x: 4, y: 4, z: 8, core: 2. Of those that a mesh axis runs over, the one named last changes fastest.
Arguments:
- tokens: bfloat16 [16384, 4096], P(('cache', 'tp')), may hold values from -6 to 6
- weight_x: bfloat16 [4096, 8192], P(None, 'tp'), may hold values from -0.09375 to 0.09375
- weight_bc: bfloat16 [4096, 2, 1024], P(None, None, 'tp'), may hold values from -0.046875 to 0.046875
- weight_dt: bfloat16 [4096, 128], P(None, 'tp'), may hold values from -0.09375 to 0.09375
- kernel_x: bfloat16 [4, 8192], P(None, 'tp'), may hold values from -3 to 3
- kernel_bc: bfloat16 [4, 2, 1024], P(None, None, 'tp'), may hold values from -3 to 3
- dt_bias: float32 [128], P('tp'), may hold values from -3 to -1
- decay_rate: float32 [128], P('tp'), may hold values from 0.05 to 8
- skip_gain: float32 [128], P('tp'), may hold values from 0.5 to 1.5
- ssm_pool: bfloat16 [64, 128, 64, 128], P('cache', 'tp'), may hold values from -2 to 2
- conv_x_pool: bfloat16 [64, 3, 8192], P('cache', None, 'tp'), may hold values from -6 to 6
- conv_bc_pool: bfloat16 [64, 3, 2, 1024], P('cache', None, None, 'tp'), may hold values from -3 to 3
- hit_holder: int32 [1024, 1], replicated, may hold values from 0 to 31; in each aligned block of 32 rows (0 to 31, 32 to 63, ...) at most 2 rows name the same one
- hit_slot: int32 [1024], replicated, may hold values from 0 to 1
- suffix_len: int32 [32, 32], P('cache'), may hold values from 1 to 32, 512 in all within a row
Outputs:
- mixed: bfloat16 [16384, 8192], P('cache', 'tp')
The draws below stay inside these ranges and needn't reach their ends.
Inputs may be any that keep to these rules, and one draw needn't show every extreme that they name: `hit_holder`: row o * 32 + k is request k of group o; among the 32 requests of one group at most 2 name the same holder, and some group reaches 2. `suffix_len`: the 32 lengths of one group sum to 512; the longest of all is exactly 32.
All inputs are finite; a program needn't handle non-finite values.
Results may differ from the reference program's by a relative error of at most 0.014.
Values may be sent and summed in bfloat16 or wider, within the bound.
No kernel may reach another device: no remote copies, remote signals or barrier semaphores. Data moves between devices by JAX's collectives and lax.ppermute only.
A program may use at most 128 MiB of HBM per device.

```python
import math
import jax
import jax.numpy as jnp
import numpy as np
from jax import lax

D = 4096
HEADS = 128
HDIM = 64
NSTATE = 128
GROUPS = 8
CONVK = 4
CAP = 2
SLOTS = 2
NREQ = 32
ROWS = 512
TOKENS = 16384
HOLDERS = 32
REQS = 1024
POOL = 64
MAXLEN = 32


def with_ends(array, rng, smallest, high):
    place = [jax.random.randint(jax.random.fold_in(rng, axis), (), 0, length) for axis, length in enumerate(array.shape)]
    longest = array.shape.index(max(array.shape))
    neighbour = place[:longest] + [(place[longest] + 1) % array.shape[longest]] + place[longest + 1:]
    return array.at[tuple(place)].set(smallest).at[tuple(neighbour)].set(high)


def shard_levels(rng, dims, shards, low, largest):
    loudness, own = 1.0, jax.random.fold_in(rng, 6)
    for dim, blocks in shards:
        heights = jnp.exp(jax.random.uniform(jax.random.fold_in(own, dim), (blocks,), jnp.float32, low / len(shards), largest / len(shards)))
        loudness = loudness * jnp.repeat(heights, dims[dim] // blocks).reshape([-1 if axis == dim else 1 for axis in range(len(dims))])
    return loudness


def length_profile(number_of, total, bound, skew):
    weights = [(1 << 20) // math.isqrt(standing ** skew) + 1 for standing in range(2, number_of + 1)]
    rest, given = total - bound - (number_of - 1), [1] * (number_of - 1)
    while rest > 0:
        movable = [i for i in range(number_of - 1) if given[i] < bound]
        mass, budget = sum([weights[i] for i in movable]), rest
        for i in movable:
            addition = min(bound - given[i], max(1, budget * weights[i] // mass), rest)
            given[i] = given[i] + addition
            rest = rest - addition
    return np.array([bound] + given)


def ragged(key, amount, total, limit, skew):
    if amount == 2:
        one = jax.random.randint(key, (), max(1, total - limit), min(limit, total - 1) + 1)
        return jnp.stack([one, total - one])
    sizes = jnp.asarray(length_profile(amount, total, limit, skew), jnp.int32)
    couples = (amount - 1) // 2
    giver, receiver = sizes[1:1 + 2 * couples:2], sizes[2:2 + 2 * couples:2]
    margin = jnp.minimum(giver - 1, limit - receiver)
    moved = jax.random.randint(jax.random.fold_in(key, 1), (couples,), 0, 1 << 20) % (margin + 1)
    sizes = sizes.at[1:1 + 2 * couples:2].set(giver - moved).at[2:2 + 2 * couples:2].set(receiver + moved)
    return sizes[jax.random.permutation(jax.random.fold_in(key, 2), amount)]


def routed_block(own_key, own, number, rows, amount, top, bound, skew):
    ranking = jax.random.permutation(own_key, amount)
    heavy_load, usual = load_shares(amount, rows * top, bound, skew, True), load_shares(amount, rows * top, bound, skew, False)
    places = jnp.arange(amount)

    def named(tallies, offset_by):
        used = int((tallies > 0).sum())
        fixed = max(1, used // 4)
        moved = fixed + (places - fixed + offset_by * (used - fixed)) % max(1, amount - fixed)
        return jnp.zeros((amount,), jnp.int32).at[ranking[jnp.where(places < fixed, places, moved)]].set(jnp.asarray(tallies, jnp.int32))

    tallies = jnp.where(number % 4 == 0, named(heavy_load, number // 4), named(usual, number - number // 4 - 1))
    mixed = jax.random.permutation(jax.random.fold_in(own, 3), amount)
    giver, sink = mixed[0:amount // 2 * 2:2], mixed[1:amount // 2 * 2:2]
    margin = jnp.minimum(tallies[giver] - 1, bound - tallies[sink]) // 2
    margin = jnp.where((giver == ranking[0]) | (sink == ranking[0]) | (tallies[sink] == 0), 0, jnp.maximum(margin, 0))
    moved = jax.random.randint(jax.random.fold_in(own, 4), (amount // 2,), 0, 1 << 20) % (margin + 1)
    tallies = tallies.at[giver].add(-moved).at[sink].add(moved)
    members = jnp.searchsorted(jnp.cumsum(tallies), jnp.arange(rows * top), side="right").astype(jnp.int32)
    table = members.reshape(top, rows).T
    table = table[jax.random.permutation(jax.random.fold_in(own, 1), rows)]
    offset_by = jax.random.randint(jax.random.fold_in(own, 2), (rows, 1), 0, top)
    return jnp.take_along_axis(table, (jnp.arange(top)[None, :] + offset_by) % top, axis=1)


def load_shares(number_of, total, reach, lean, full):
    portions = [(1 << 20) // math.isqrt(rank ** lean) + 1 for rank in range(1, number_of + 1)]
    largest = reach if full else min(reach, max(-(-total // number_of), total * portions[0] // sum(portions)))
    least = 1 if total - largest >= number_of - 1 else 0
    holding, rest = [largest] + [least] * (number_of - 1), total - largest - least * (number_of - 1)
    while rest > 0:
        candidates = [i for i in range(1, number_of) if holding[i] < largest] or [i for i in range(1, number_of) if holding[i] < reach]
        mass, left = sum([portions[i] for i in candidates]), rest
        for i in candidates:
            extra = min(reach - holding[i], max(1, left * portions[i] // mass), rest)
            holding[i] = holding[i] + extra
            rest = rest - extra
    return np.array(holding)


def noise(key, dims, deviation, limit, pieces=(), held_as=jnp.bfloat16):
    result = jax.random.normal(key, dims, jnp.float32) * deviation
    if len(pieces) > 0:
        result = shard_levels(key, dims, pieces, -0.22, 0.18) * result
    return jnp.clip(result, min=-limit, max=limit).astype(held_as)


def setup_inputs(seed: int = 0) -> dict:
    keys = jax.random.split(jax.random.key(seed), 16)
    tokens = noise(keys[0], (TOKENS, D), 1.0, 6.0, ((0, 256),))
    weight_x = noise(keys[1], (D, HEADS * HDIM), D ** -0.5, 0.09375, ((1, 8),))
    weight_bc = noise(keys[2], (D, 2, GROUPS * NSTATE), (0.5 * D ** -0.5), 0.046875, ((2, 8),))
    weight_dt = noise(keys[3], (D, HEADS), D ** -0.5, 0.09375, ((1, 8),))
    kernel_x = noise(keys[4], (CONVK, HEADS * HDIM), CONVK ** -0.5, 3.0, ((1, 8),))
    kernel_bc = noise(keys[5], (CONVK, 2, GROUPS * NSTATE), CONVK ** -0.5, 3.0, ((2, 8),))
    dt_bias = jnp.clip(-3.0 + 2.0 * jax.random.uniform(keys[6], (HEADS,), jnp.float32) ** shard_levels(keys[6], (HEADS,), ((0, 8),), -0.2, 0.2), -3.0, -1.0)
    decay_rate = jnp.clip(jnp.exp(math.log(8.0) - 5.075174 * jax.random.uniform(keys[7], (HEADS,), jnp.float32) ** shard_levels(keys[7], (HEADS,), ((0, 8),), -0.2, 0.2)), 0.05, 8.0)
    skip_gain = jnp.clip(0.5 + 1.0 * jax.random.uniform(keys[8], (HEADS,), jnp.float32) ** shard_levels(keys[8], (HEADS,), ((0, 8),), -0.2, 0.2), 0.5, 1.5)
    ssm_pool = noise(keys[9], (POOL, HEADS, HDIM, NSTATE), 0.3, 2.0, ((0, 32), (1, 8)))
    conv_x_pool = noise(keys[10], (POOL, CONVK - 1, HEADS * HDIM), 1.0, 6.0, ((0, 32), (2, 8)))
    conv_bc_pool = noise(keys[11], (POOL, CONVK - 1, 2, GROUPS * NSTATE), 0.5, 3.0, ((0, 32), (3, 8)))
    hit_holder_keys = jax.random.split(jax.random.fold_in(keys[12], 1), REQS // NREQ)
    hit_holder_turns = jax.random.permutation(jax.random.fold_in(keys[12], 3), REQS // NREQ)
    hit_holder = jax.vmap(lambda own, number: routed_block(jax.random.fold_in(keys[12], 2), own, number, NREQ, HOLDERS, 1, CAP, 2))(hit_holder_keys, hit_holder_turns).reshape((REQS, 1))
    hit_slot = with_ends(jax.random.randint(keys[13], (REQS,), 0, SLOTS), jax.random.fold_in(keys[13], 1), 0, SLOTS - 1).astype(jnp.int32)
    suffix_len = jax.vmap(lambda own: ragged(own, NREQ, ROWS, MAXLEN, 2))(jax.random.split(keys[14], HOLDERS)).reshape((HOLDERS, NREQ)).astype(jnp.int32)
    return {"tokens": tokens, "weight_x": weight_x, "weight_bc": weight_bc, "weight_dt": weight_dt, "kernel_x": kernel_x, "kernel_bc": kernel_bc, "dt_bias": dt_bias, "decay_rate": decay_rate, "skip_gain": skip_gain, "ssm_pool": ssm_pool, "conv_x_pool": conv_x_pool, "conv_bc_pool": conv_bc_pool, "hit_holder": hit_holder, "hit_slot": hit_slot, "suffix_len": suffix_len}


def request_layout(lengths, row_count):
    end_rows = jnp.cumsum(lengths).astype(jnp.int32)
    starts = (end_rows - lengths).astype(jnp.int32)
    position = jnp.arange(row_count, dtype=jnp.int32)
    req_of = jnp.sum((position[:, None] >= end_rows[None, :]).astype(jnp.int32), axis=1).astype(jnp.int32)
    onehot = (req_of[:, None] == jnp.arange(lengths.shape[0], dtype=jnp.int32)[None, :]).astype(jnp.int32)
    offset = (position - jnp.sum(onehot * starts[None, :], axis=1)).astype(jnp.int32)
    return starts, req_of, offset


def causal_conv(inputs, states, kernel, req_of, offset):
    kernel_taps = kernel.shape[0]
    row_count = inputs.shape[0]
    flat_states = states.reshape((states.shape[0] * (kernel_taps - 1),) + states.shape[2:])
    unit_dims = (1,) * (inputs.ndim - 1)
    summed = kernel[kernel_taps - 1].astype(jnp.float32) * inputs.astype(jnp.float32)
    for lag_steps in range(1, kernel_taps):
        shifted = jnp.concatenate([jnp.zeros((lag_steps,) + inputs.shape[1:], inputs.dtype), inputs[:row_count - lag_steps]], axis=0)
        state_row = (req_of * (kernel_taps - 1) + jnp.clip(kernel_taps - 1 - lag_steps + offset, 0, kernel_taps - 2)).astype(jnp.int32)
        from_state = jnp.take(flat_states, state_row, axis=0)
        inside = (offset < lag_steps).reshape((row_count,) + unit_dims)
        chosen_vals = jnp.where(inside, from_state, shifted)
        summed = summed + kernel[kernel_taps - 1 - lag_steps].astype(jnp.float32) * chosen_vals.astype(jnp.float32)
    return jax.nn.silu(summed).astype(jnp.bfloat16)


def one_group(rows_in, weight_x, weight_bc, weight_dt, kernel_x, kernel_bc, dt_bias, decay_rate, skip_gain, states, conv_x_prior, conv_bc_prior, lengths):
    row_count = rows_in.shape[0]
    model_dim = rows_in.shape[1]
    head_count = weight_dt.shape[1]
    head_size = weight_x.shape[1] // head_count
    group_state = weight_bc.shape[2]
    state_size = states.shape[3]
    group_count = group_state // state_size
    per_group = head_count // group_count
    req_count = lengths.shape[0]
    max_len = 2 * row_count // req_count
    x_in = jnp.dot(rows_in, weight_x, preferred_element_type=jnp.float32).astype(jnp.bfloat16)
    bc_in = jnp.dot(rows_in, weight_bc.reshape(model_dim, 2 * group_state), preferred_element_type=jnp.float32).astype(jnp.bfloat16)
    bc_in = bc_in.reshape(row_count, 2, group_state)
    dt_in = jnp.dot(rows_in, weight_dt, preferred_element_type=jnp.float32).astype(jnp.bfloat16)
    starts, req_of, offset = request_layout(lengths, row_count)
    x_conv = causal_conv(x_in, conv_x_prior, kernel_x, req_of, offset)
    bc_conv = causal_conv(bc_in, conv_bc_prior, kernel_bc, req_of, offset)
    b_rows = bc_conv[:, 0].reshape(row_count, group_count, state_size)
    c_rows = bc_conv[:, 1].reshape(row_count, group_count, state_size)
    step_size = jax.nn.softplus(dt_in.astype(jnp.float32) + dt_bias[None, :])
    log_keep = -step_size * decay_rate[None, :]
    running = jnp.cumsum(log_keep, axis=0)
    position = jnp.arange(row_count, dtype=jnp.int32)
    values = x_conv.reshape(row_count, head_count, head_size)
    window_start = jnp.clip(starts, 0, row_count - max_len).astype(jnp.int32)
    window_rows = (window_start[:, None] + jnp.arange(max_len, dtype=jnp.int32)[None, :]).reshape(-1)
    run_w = jnp.take(running, window_rows, axis=0).reshape(req_count, max_len, head_count)
    step_w = jnp.take(step_size, window_rows, axis=0).reshape(req_count, max_len, head_count)
    b_w = jnp.take(b_rows, window_rows, axis=0).reshape(req_count, max_len, group_count, state_size)
    c_w = jnp.take(c_rows, window_rows, axis=0).reshape(req_count, max_len, group_count, state_size)
    x_w = jnp.take(values, window_rows, axis=0).reshape(req_count, max_len, head_count, head_size)
    req_w = jnp.take(req_of, window_rows, axis=0).reshape(req_count, max_len)
    pos_w = window_rows.reshape(req_count, max_len)
    req_ids = jnp.arange(req_count, dtype=jnp.int32)
    valid = (req_w[:, :, None] == req_ids[:, None, None]) & (req_w[:, None, :] == req_ids[:, None, None]) & (pos_w[:, :, None] >= pos_w[:, None, :])
    score_w = jnp.einsum("qmgn,qsgn->qgms", c_w.astype(jnp.float32), b_w.astype(jnp.float32))
    run_t = run_w.transpose(0, 2, 1).reshape(req_count, group_count, per_group, max_len)
    step_t = step_w.transpose(0, 2, 1).reshape(req_count, group_count, per_group, 1, max_len)
    log_gap = run_t[:, :, :, :, None] - run_t[:, :, :, None, :]
    mixing = jnp.exp(jnp.where(valid[:, None, None], log_gap, -jnp.inf)) * score_w[:, :, None] * step_t
    mixing = mixing.astype(jnp.bfloat16).reshape(req_count, head_count, max_len, max_len)
    inner_w = jnp.einsum("qhms,qshd->qmhd", mixing.astype(jnp.float32), x_w.astype(jnp.float32))
    c_heads = jnp.broadcast_to(c_w[:, :, :, None, :], (req_count, max_len, group_count, per_group, state_size)).reshape(req_count, max_len, head_count, state_size)
    carried = jnp.einsum("qmhn,qhdn->qmhd", c_heads.astype(jnp.float32), states.astype(jnp.float32))
    pick_row = (req_of * max_len + position - jnp.take(window_start, req_of, axis=0)).astype(jnp.int32)
    inner_term = jnp.take(inner_w.reshape(req_count * max_len, head_count, head_size), pick_row, axis=0)
    carried_rows = jnp.take(carried.reshape(req_count * max_len, head_count, head_size), pick_row, axis=0)
    base_log = jnp.take(running - log_keep, starts, axis=0)
    fade_out = jnp.exp(running - jnp.take(base_log, req_of, axis=0))
    summed = inner_term + fade_out[:, :, None] * carried_rows + skip_gain[None, :, None] * values.astype(jnp.float32)
    return summed.reshape(row_count, head_count * head_size).astype(jnp.bfloat16)


def reference(tokens, weight_x, weight_bc, weight_dt, kernel_x, kernel_bc, dt_bias, decay_rate, skip_gain, ssm_pool, conv_x_pool, conv_bc_pool, hit_holder, hit_slot, suffix_len):
    def per_owner(owner_id):
        rows_in = lax.dynamic_slice_in_dim(tokens, owner_id * ROWS, ROWS, 0)
        holders = lax.dynamic_slice_in_dim(hit_holder[:, 0], owner_id * NREQ, NREQ, 0)
        slots = lax.dynamic_slice_in_dim(hit_slot, owner_id * NREQ, NREQ, 0)
        pool_rows = (holders * SLOTS + slots).astype(jnp.int32)
        states = jnp.take(ssm_pool, pool_rows, axis=0)
        conv_x_prior = jnp.take(conv_x_pool, pool_rows, axis=0)
        conv_bc_prior = jnp.take(conv_bc_pool, pool_rows, axis=0)
        lengths = lax.dynamic_index_in_dim(suffix_len, owner_id, 0, keepdims=False)
        return one_group(rows_in, weight_x, weight_bc, weight_dt, kernel_x, kernel_bc, dt_bias, decay_rate, skip_gain, states, conv_x_prior, conv_bc_prior, lengths)

    outputs = lax.map(per_owner, jnp.arange(HOLDERS, dtype=jnp.int32))
    return outputs.reshape(TOKENS, HEADS * HDIM)
```

```python
import jax
import jax.numpy as jnp
from jax import lax
from jax.experimental import pallas as pl
from jax.experimental.pallas import tpu as pltpu
from jax.sharding import PartitionSpec as P

NX, NY, NZ = 4, 4, 8
TILE = 64
F32, BF16 = jnp.float32, jnp.bfloat16


def chip(y, x, c):
    return (y % NY) * 2 * NX + (x % NX) * 2 + c


def every():
    return [(y, x, c) for y in range(NY) for x in range(NX) for c in range(2)]


RING_X = [(chip(y, x, c), chip(y, x + 1 - 2 * c, c)) for y, x, c in every()]
RING_Y = [(chip(y, x, c), chip(y + 1 - 2 * c, x, c)) for y, x, c in every()]
CORES = [(chip(y, x, c), chip(y, x, 1 - c)) for y, x, c in every()]


def over_z(value, step):
    return lax.ppermute(value, "tp", [(z, (z + step) % NZ) for z in range(NZ)])


def on_cache(value, pairs):
    return lax.ppermute(value, "cache", pairs)


def gather_pool(pool):
    rows = pool.shape[0] // 2
    first, second = pool[:rows], pool[rows:]
    along_x, along_y = [first], [second]
    for _ in range(NX - 1):
        first = on_cache(first, RING_X)
        second = on_cache(second, RING_Y)
        along_x.append(first)
        along_y.append(second)
    first, second = jnp.concatenate(along_x), jnp.concatenate(along_y)
    firsts, seconds = [first], [second]
    for _ in range(NX - 1):
        first = on_cache(first, RING_Y)
        second = on_cache(second, RING_X)
        firsts.append(first)
        seconds.append(second)
    own = firsts + seconds
    return own + [on_cache(part, CORES) for part in own]


def dot(a, b):
    return jnp.dot(a, b, preferred_element_type=F32)


def dot_t(a, b):
    return lax.dot_general(a, b, (((1,), (1,)), ((), ())), preferred_element_type=F32)


def inner_kernel(
    where, px0, px1, px2, px3, px4, pb0, pb1, pb2, pb3, pb4, meta, req_row, req_win, prior, taps, bias,
    decay, skip, part_ref, c_ref, fade_ref, raw, xs, bs, cs, run, step,
):
    rows = req_row.shape[1]
    x_cols = part_ref.shape[1]
    cols = prior.shape[1]
    block = rows // NZ
    z = where[0]
    raw[0:8, :] = jnp.zeros((8, cols), F32)

    def place(source, first, x_part, b_part):
        at = pl.multiple_of(lax.rem(source + NZ, NZ) * block, block)
        raw[pl.ds(8 + at, block), 0:x_cols] = x_part[first : first + block, :].astype(F32)
        raw[pl.ds(8 + at, block), x_cols:cols] = b_part[
            first : first + block, 0 : cols - x_cols
        ].astype(F32)
        step[pl.ds(TILE + at, block), :] = b_part[
            first : first + block, cols - x_cols : cols - x_cols + 128
        ].astype(F32)

    place(z, 0, px0, pb0)
    for k, (x_part, b_part) in enumerate(((px1, pb1), (px2, pb2), (px3, pb3)), 1):
        place(z - k, 0, x_part, b_part)
        place(z + k, block, x_part, b_part)
    place(z + 4, 0, px4, pb4)

    req_col, offset, base = meta[:, 0:1], meta[:, 1:2], meta[:, 2:3]
    steps = jax.nn.softplus(step[TILE:, :] + bias[...])
    step[0:TILE, :] = jnp.zeros((TILE, 128), F32)
    step[TILE:, :] = steps
    log_keep = -steps * decay[...]
    before = lax.broadcasted_iota(jnp.int32, (rows, rows), 0) >= lax.broadcasted_iota(
        jnp.int32, (rows, rows), 1
    )
    sums = jnp.where((req_col == req_row[...]) & before, 1.0, 0.0).astype(BF16)
    high = log_keep.astype(BF16)
    rest = log_keep - high.astype(F32)
    middle = rest.astype(BF16)
    low = (rest - middle.astype(F32)).astype(BF16)
    running = dot(sums, high) + dot(sums, middle) + dot(sums, low)
    run[0:TILE, :] = jnp.zeros((TILE, 128), F32)
    run[TILE:, :] = running
    fade_ref[...] = jnp.exp(running)
    xs[0:TILE, :] = jnp.zeros((TILE, x_cols), BF16)
    bs[0:TILE, :] = jnp.zeros((TILE, 128), BF16)
    c_ref[rows:, :] = jnp.zeros((c_ref.shape[0] - rows, 128), F32)
    slot_ids = lax.broadcasted_iota(jnp.int32, (rows, prior.shape[0]), 1)
    chosen = [
        jnp.where((slot_ids == base + offset + (3 - lag)) & (offset < lag), 1.0, 0.0).astype(BF16)
        for lag in (1, 2, 3)
    ]
    width = 256
    for at in range(0, cols, width):
        here = slice(at, at + width)
        total = taps[3:4, here] * raw[8 : 8 + rows, here]
        for lag in (1, 2, 3):
            shifted = raw[8 - lag : 8 - lag + rows, here]
            value = jnp.where(offset < lag, 0.0, shifted) + dot(chosen[lag - 1], prior[:, here])
            total = total + taps[3 - lag : 4 - lag, here] * value
        out = (total / (1.0 + jnp.exp(-total))).astype(BF16)
        if at < x_cols:
            xs[TILE:, here] = out
        else:
            bs[TILE:, :] = out[:, 0:128]
            cs[...] = out[:, 128:256]
            c_ref[0:rows, :] = out[:, 128:256].astype(F32)

    lanes = lax.broadcasted_iota(jnp.int32, (TILE, 2 * TILE), 1)
    subs = lax.broadcasted_iota(jnp.int32, (TILE, 2 * TILE), 0)
    quarter = lax.broadcasted_iota(jnp.int32, (TILE, 4 * TILE), 1) // TILE

    def tile(j, carry):
        at = pl.multiple_of(j * TILE, TILE)
        score = dot_t(cs[pl.ds(at, TILE), :], bs[pl.ds(at, 2 * TILE), :])
        mask = (meta[pl.ds(at, TILE), 0:1] == req_win[pl.ds(j, 1), :]) & (lanes - TILE <= subs)
        run_w = run[pl.ds(at, 2 * TILE), :]
        run_rows = run_w.T
        step_rows = step[pl.ds(at, 2 * TILE), :].T
        run_cols = run_w[TILE:, :]
        for group in range(x_cols // (4 * TILE)):
            mixes = []
            for h in range(4 * group, 4 * group + 4):
                gap = run_cols[:, h : h + 1] - run_rows[h : h + 1, :]
                mix = jnp.exp(jnp.where(mask, gap, -jnp.inf)) * score * step_rows[h : h + 1, :]
                mixes.append(mix.astype(BF16))
            here = slice(4 * TILE * group, 4 * TILE * (group + 1))
            x_w = xs[pl.ds(at, 2 * TILE), here]
            product = dot(jnp.concatenate(mixes, axis=0), x_w)
            out = product[0:TILE]
            for i in range(1, 4):
                out = jnp.where(quarter == i, product[i * TILE : (i + 1) * TILE], out)
            part_ref[pl.ds(at, TILE), here] = out + skip[:, here] * x_w[TILE:].astype(F32)
        return carry

    lax.fori_loop(0, rows // TILE, tile, 0)


def carried_kernel(table, *refs):
    arrays, (part, c_ref, fade, out, states, carried, sems) = refs[:16], refs[16:]
    rows, x_cols = out.shape
    requests = states.shape[0]

    def begin(r, carry):
        for k, array in enumerate(arrays):

            @pl.when(table[1, r] == k)
            def _():
                at = pl.multiple_of(table[2, r] * x_cols, x_cols)
                pltpu.make_async_copy(array.at[pl.ds(at, x_cols), :], states.at[r], sems.at[r]).start()

        return carry

    lax.fori_loop(0, requests, begin, 0)

    def one(r, carry):
        pltpu.make_async_copy(
            arrays[0].at[pl.ds(0, x_cols), :], states.at[r], sems.at[r]
        ).wait()
        start = table[0, r]
        window = c_ref[pl.ds(start, 32), :].astype(BF16)
        product = dot_t(window, states[r])
        for k in range(x_cols // 128):
            carried[k, pl.ds(start, 32), :] = product[:, 128 * k : 128 * (k + 1)]
        return carry

    lax.fori_loop(0, requests, one, 0)
    left = lax.broadcasted_iota(jnp.int32, (TILE, 128), 1) < 64
    for at in range(0, rows, TILE):
        here = slice(at, at + TILE)
        for pair in range(x_cols // 128):
            cols = slice(128 * pair, 128 * (pair + 1))
            scale = jnp.where(
                left, fade[here, 2 * pair : 2 * pair + 1], fade[here, 2 * pair + 1 : 2 * pair + 2]
            )
            out[here, cols] = (part[here, cols] + scale * carried[pair, here, :]).astype(BF16)


def mixer_inner(z, px, pb, meta, req_row, req_win, prior, taps, bias, decay, skip):
    rows, x_cols, cols = req_row.shape[1], px[0].shape[1], prior.shape[1]
    vmem = pl.BlockSpec(memory_space=pltpu.VMEM)
    return pl.pallas_call(
        inner_kernel,
        out_shape=(
            jax.ShapeDtypeStruct((rows, x_cols), F32),
            jax.ShapeDtypeStruct((rows + 32, 128), F32),
            jax.ShapeDtypeStruct((rows, 128), F32),
        ),
        in_specs=[pl.BlockSpec(memory_space=pltpu.SMEM)] + [vmem] * 18,
        out_specs=(vmem, vmem, vmem),
        scratch_shapes=[
            pltpu.VMEM((rows + 8, cols), F32),
            pltpu.VMEM((rows + TILE, x_cols), BF16),
            pltpu.VMEM((rows + TILE, 128), BF16),
            pltpu.VMEM((rows, 128), BF16),
            pltpu.VMEM((rows + TILE, 128), F32),
            pltpu.VMEM((rows + TILE, 128), F32),
        ],
        compiler_params=pltpu.CompilerParams(vmem_limit_bytes=32 * 1024 * 1024),
        cost_estimate=pl.CostEstimate(flops=2000000000, bytes_accessed=8000000, transcendentals=2000000),
        name="mixer_inner",
    )(z, *px, *pb, meta, req_row, req_win, prior, taps, bias, decay, skip)


def mixer_carried(table, arrays, part, c_rows, fade):
    rows, x_cols = part.shape
    requests = table.shape[1]
    vmem = pl.BlockSpec(memory_space=pltpu.VMEM)
    return pl.pallas_call(
        carried_kernel,
        out_shape=jax.ShapeDtypeStruct((rows, x_cols), BF16),
        in_specs=[pl.BlockSpec(memory_space=pltpu.SMEM)]
        + [pl.BlockSpec(memory_space=pl.ANY)] * 16
        + [vmem] * 3,
        out_specs=vmem,
        scratch_shapes=[
            pltpu.VMEM((requests, x_cols, 128), BF16),
            pltpu.VMEM((x_cols // 128, rows + 32, 128), F32),
            pltpu.SemaphoreType.DMA((requests,)),
        ],
        compiler_params=pltpu.CompilerParams(vmem_limit_bytes=32 * 1024 * 1024),
        cost_estimate=pl.CostEstimate(flops=500000000, bytes_accessed=13000000, transcendentals=0),
        name="mixer_carried",
    )(table, *arrays, part, c_rows, fade)


def shards(
    tokens, weight_x, weight_bc, weight_dt, kernel_x, kernel_bc, dt_bias, decay_rate, skip_gain,
    ssm_pool, conv_x_pool, conv_bc_pool, hit_holder, hit_slot, suffix_len,
):
    model_dim, heads = weight_dt.shape
    x_cols = weight_x.shape[1]
    bc_cols = weight_bc.shape[1] * weight_bc.shape[2]
    slots, head_size, state_size = ssm_pool.shape[0], ssm_pool.shape[2], ssm_pool.shape[3]
    requests = suffix_len.shape[1]
    rows = NZ * tokens.shape[0]
    me, z = lax.axis_index("cache"), lax.axis_index("tp")

    prior = jnp.concatenate([conv_x_pool, conv_bc_pool.reshape(slots, 3, bc_cols)], axis=2)
    prior = jnp.pad(prior.reshape(slots * 3, x_cols + bc_cols), ((0, 8 - slots * 3), (0, 0)))
    holders = 2 * NX * NY
    prior = lax.all_to_all(
        jnp.broadcast_to(prior[None], (holders,) + prior.shape), "cache", 0, 0, tiled=True
    ).reshape(holders * 8, x_cols + bc_cols)

    arrays = gather_pool(ssm_pool.reshape(slots * heads * head_size, state_size))

    weight_rest = jnp.concatenate(
        [weight_bc.reshape(model_dim, bc_cols), jnp.pad(weight_dt, ((0, 0), (0, 128 - heads)))], axis=1
    )

    def project(block):
        return dot(block, weight_x).astype(BF16), dot(block, weight_rest).astype(BF16)

    half = tokens.shape[0] // 2
    up = down = tokens
    parts = [project(tokens)]
    for _ in range(3):
        up, down = over_z(up, 1), over_z(down, -1)
        parts.append(project(jnp.concatenate([up, down])))
    up, down = over_z(up[:half], 1), over_z(down[half:], -1)
    parts.append(project(jnp.concatenate([up, down])))

    lengths = suffix_len[0]
    ends = jnp.cumsum(lengths)
    starts = ends - lengths
    position = jnp.arange(rows, dtype=jnp.int32)
    req_of = jnp.sum((position[:, None] >= ends[None, :]).astype(jnp.int32), axis=1)
    onehot = (req_of[:, None] == jnp.arange(requests)[None, :]).astype(jnp.int32)
    holder = lax.dynamic_slice_in_dim(hit_holder[:, 0], me * requests, requests)
    slot = lax.dynamic_slice_in_dim(hit_slot, me * requests, requests)
    offset = position - jnp.sum(onehot * starts[None, :], axis=1)
    base = jnp.sum(onehot * (holder * 8 + slot * 3)[None, :], axis=1)
    meta = jnp.stack([req_of, offset, base, base], axis=1)
    padded = jnp.concatenate([jnp.full((TILE,), -1, jnp.int32), req_of]).reshape(-1, TILE)
    req_win = jnp.concatenate([padded[:-1], padded[1:]], axis=1)

    my_y, my_x, my_c = me // (2 * NX), (me // 2) % NX, me % 2
    at_y, at_x, at_c = holder // (2 * NX), (holder // 2) % NX, holder % 2
    sign = 1 - 2 * at_c
    far_y, far_x = ((my_y - at_y) * sign) % NY, ((my_x - at_x) * sign) % NX
    array = jnp.where(at_c == my_c, 0, 8) + slot * 4 + jnp.where(slot == 0, far_y, far_x)
    table = jnp.stack([starts, array, jnp.where(slot == 0, far_x, far_y)]).astype(jnp.int32)

    taps = jnp.concatenate([kernel_x, kernel_bc.reshape(4, bc_cols)], axis=1).astype(F32)
    pad = (0, 128 - heads)
    part, c_rows, fade = mixer_inner(
        z.reshape(1), [p[0] for p in parts], [p[1] for p in parts], meta, req_of[None, :], req_win, prior, taps,
        jnp.pad(dt_bias, pad)[None], jnp.pad(decay_rate, pad)[None], jnp.repeat(skip_gain, head_size)[None],
    )
    return mixer_carried(table, arrays, part, c_rows, fade)


def solution(mesh):
    in_specs = (
        P(("cache", "tp"), None), P(None, "tp"), P(None, None, "tp"), P(None, "tp"), P(None, "tp"),
        P(None, None, "tp"), P("tp"), P("tp"), P("tp"), P("cache", "tp", None, None), P("cache", None, "tp"),
        P("cache", None, None, "tp"), P(), P(), P("cache", None),
    )
    return jax.shard_map(
        shards, mesh=mesh, in_specs=in_specs, out_specs=P("cache", "tp"), check_vma=False
    )
```

```python
import jax
import jax.numpy as jnp
from jax import lax
from jax.experimental import pallas as pl
from jax.experimental.pallas import tpu as pltpu
from jax.sharding import PartitionSpec as P

NX, NY, NZ = 4, 4, 8
MOST = 60 * 1024 * 1024
TILE = 64
PRIOR = 16
PRIORS = NX * PRIOR
WIDE = 512
F32, BF16 = jnp.float32, jnp.bfloat16


def chip(y, x, c):
    return (y % NY) * 2 * NX + (x % NX) * 2 + c


def every():
    return [(y, x, c) for y in range(NY) for x in range(NX) for c in range(2)]


def first_round(step):
    return [(chip(y, x, c), chip(y + c * step, x + (1 - c) * step, c)) for y, x, c in every()]


def second_round(step):
    return [(chip(y, x, c), chip(y + (1 - c) * step, x + c * step, c)) for y, x, c in every()]


CORES = [(chip(y, x, c), chip(y, x, 1 - c)) for y, x, c in every()]


def over_z(value, step):
    return lax.ppermute(value, "tp", [(z, (z + step) % NZ) for z in range(NZ)])


def on_cache(value, pairs):
    return lax.ppermute(value, "cache", pairs)


def moved(name, sources, shapes, moves):
    def kernel(*refs):
        ins, (outs, held, sems) = refs[: len(sources)], (refs[len(sources) : -2], refs[-2], refs[-1])
        inward, outward, first = [], [], 0
        for k, (src, at, count, dst, to) in enumerate(moves):
            spot = held.at[pl.ds(first, count), :]
            inward.append(pltpu.make_async_copy(ins[src].at[pl.ds(at, count), :], spot, sems.at[2 * k]))
            outward.append(pltpu.make_async_copy(spot, outs[dst].at[pl.ds(to, count), :], sems.at[2 * k + 1]))
            first += count
        for copy in inward:
            copy.start()
        for before, after in zip(inward, outward):
            before.wait()
            after.start()
        for copy in outward:
            copy.wait()

    rows = sum(move[2] for move in moves)
    return pl.pallas_call(
        kernel,
        out_shape=[jax.ShapeDtypeStruct(shape, sources[0].dtype) for shape in shapes],
        in_specs=[pl.BlockSpec(memory_space=pltpu.HBM)] * len(sources),
        out_specs=[pl.BlockSpec(memory_space=pltpu.HBM)] * len(shapes),
        scratch_shapes=[
            pltpu.VMEM((rows, sources[0].shape[1]), sources[0].dtype),
            pltpu.SemaphoreType.DMA((2 * len(moves),)),
        ],
        compiler_params=pltpu.CompilerParams(vmem_limit_bytes=MOST),
        cost_estimate=pl.CostEstimate(flops=0, bytes_accessed=4000000, transcendentals=0),
        name=name,
    )(*sources)


def lined(nodes):
    states, cols = nodes[0].shape[0] - PRIOR, nodes[0].shape[1]
    moves = []
    for k in range(len(nodes)):
        moves.append((k, 0, states, 0, k * states))
        moves.append((k, states, PRIOR, 1, k * PRIOR))
    return moved("lined", nodes, [(len(nodes) * states, cols), (len(nodes) * PRIOR, cols)], moves)


def stacked(parts):
    rows, cols = parts[0].shape
    moves = [(k, 0, rows, 0, k * rows) for k in range(len(parts))]
    return moved("stacked", parts, [(len(parts) * rows, cols)], moves)[0]


def halves(top, bottom):
    rows, cols = top.shape[0] // 2, top.shape[1]
    return moved("halves", [top, bottom], [(rows, cols)] * 2, [(0, 0, rows, 0, 0), (1, rows, rows, 1, 0)])


def gather(pool, tokens, tables, project, inner):
    tie = lax.optimization_barrier
    near_up, near_down = on_cache(pool, first_round(1)), on_cache(pool, first_round(-1))
    far = on_cache(pool, first_round(2))
    up, down = over_z(tokens, 1), over_z(tokens, -1)
    near_up, near_down, far, up, down, tables = tie((near_up, near_down, far, up, down, tables))

    blocks = [tokens, up, down]
    up, down = over_z(up, 1), over_z(down, -1)
    blocks += [up, down]
    line, line_prior = lined([pool, near_up, near_down, far])
    priors = [line_prior] + [on_cache(line_prior, second_round(step)) for step in (1, -1, 2)]
    line, priors = tie((line, priors))
    near_up, near_down = on_cache(line, second_round(1)), on_cache(line, second_round(-1))
    priors = stacked(priors)
    priors = [priors, on_cache(priors, CORES)]
    line_other = on_cache(line, CORES)
    blocks, line_other, priors = tie((blocks, line_other, priors))
    projected = project(blocks, tables[1])
    up, down = over_z(up, 1), over_z(down, -1)
    blocks = [up, down]
    near_up, near_down, up, down, projected = tie((near_up, near_down, up, down, projected))

    last_up, last_down = halves(up, down)
    blocks += [over_z(last_up, 1), over_z(last_down, -1)]
    far_up, far_down = halves(near_up, near_down)
    far_up, far_down = on_cache(far_up, second_round(1)), on_cache(far_down, second_round(-1))
    up_other, down_other, blocks = tie((near_up, near_down, blocks))
    up_other, down_other = on_cache(up_other, CORES), on_cache(down_other, CORES)
    result = inner(blocks, projected, [line, line_other, near_up, near_down], priors, tables)
    far_up, far_down, result = tie((far_up, far_down, result))
    far_others = [on_cache(far_up, CORES), on_cache(far_down, CORES)]
    return [up_other, down_other, far_up, far_others[0], far_down, far_others[1]], result


def dot(a, b):
    return jnp.dot(a, b, preferred_element_type=F32)


def dot_t(a, b):
    return lax.dot_general(a, b, (((1,), (1,)), ((), ())), preferred_element_type=F32)


def fetched(blocks, weights, tok, held, sem):
    w_x_in, w_bc_in, w_dt_in = weights
    w_x, w_bc, w_dt = held
    now, at = [], 0
    for block in blocks:
        now.append(pltpu.make_async_copy(block, tok.at[pl.ds(at, block.shape[0]), :], sem.at[len(now)]))
        at += block.shape[0]
    heads = w_dt_in.shape[0]
    now.append(pltpu.make_async_copy(w_bc_in, w_bc, sem.at[len(now)]))
    now.append(pltpu.make_async_copy(w_dt_in, w_dt.at[pl.ds(0, heads), :], sem.at[len(now)]))
    chunks = []
    for k in range(w_x.shape[1] // WIDE):
        here = (slice(None), slice(WIDE * k, WIDE * (k + 1)))
        chunks.append(pltpu.make_async_copy(w_x_in.at[here], w_x.at[here], sem.at[len(now) + k]))
    for copy in now + chunks:
        copy.start()
    w_dt[heads:, :] = jnp.zeros((128 - heads, w_dt.shape[1]), BF16)
    return now, chunks


def project_kernel(*refs):
    blocks, (w_x_in, w_bc_in, w_dt_in, x_out, b_out, tok, w_x, w_bc, w_dt, sem) = refs[:-10], refs[-10:]
    now, chunks = fetched(blocks, (w_x_in, w_bc_in, w_dt_in), tok, (w_x, w_bc, w_dt), sem)
    for copy in now:
        copy.wait()
    b_out[:, 0:256] = dot(tok[...], w_bc[...]).astype(BF16)
    b_out[:, 256:384] = dot_t(tok[...], w_dt[...]).astype(BF16)
    for k, copy in enumerate(chunks):
        copy.wait()
        here = slice(WIDE * k, WIDE * (k + 1))
        x_out[:, here] = dot(tok[...], w_x[:, here]).astype(BF16)


def inner_kernel(
    where, table, b0, b1, b2, b3, w_x_in, w_bc_in, w_dt_in, s0, s1, s2, s3, p0, p1,
    x_first, b_first, info, cols_in, taps, bias, decay, skip, sum_ref, c_ref, fade_ref,
    raw, xs, bs, cs, run, step, tok, w_x, w_bc, w_dt, sem, states, state_sem, prior, prior_sem,
):
    rows = raw.shape[0] - 8
    x_cols = w_x.shape[1]
    cols = taps.shape[1]
    block = rows // NZ
    z = where[0]
    now, chunks = fetched([b0, b1, b2, b3], (w_x_in, w_bc_in, w_dt_in), tok, (w_x, w_bc, w_dt), sem)
    parts = (s0, s1, s2, s3)
    fetch_states(table, 0, parts, states, state_sem)
    for k, source in enumerate((p0, p1)):
        spot = prior.at[pl.ds(k * p0.shape[0], p0.shape[0]), :]
        now.append(pltpu.make_async_copy(source, spot, prior_sem.at[k]))
        now[-1].start()

    def put(target, lead, columns, values, shifts):
        for k, shift in enumerate(shifts):
            at = pl.multiple_of(lax.rem(z + shift + NZ, NZ) * block, block)
            target[pl.ds(lead + at, block), columns] = values[k * block : (k + 1) * block].astype(F32)

    put(raw, 8, slice(0, x_cols), x_first, (0, -1, 1, -2, 2))
    put(raw, 8, slice(x_cols, cols), b_first[:, 0:256], (0, -1, 1, -2, 2))
    put(step, TILE, slice(None), b_first[:, 256:384], (0, -1, 1, -2, 2))
    raw[0:8, :] = jnp.zeros((8, cols), F32)

    position = lax.broadcasted_iota(jnp.int32, (rows, 128), 0)
    request = lax.broadcasted_iota(jnp.int32, (rows, 128), 1).astype(F32)
    req_col = jnp.sum(jnp.where(position >= info[0:1, :], 1.0, 0.0), axis=1, keepdims=True)
    is_own = request == req_col
    own_start = jnp.sum(jnp.where(is_own, info[1:2, :].astype(F32), 0.0), axis=1, keepdims=True)
    offset = position[:, 0:1].astype(F32) - own_start

    def requests_at(first, count):
        spot = first + lax.broadcasted_iota(jnp.int32, (info.shape[1], count), 1)
        found = jnp.sum(jnp.where(spot >= cols_in[:, 1:2], 1.0, 0.0), axis=0, keepdims=True)
        return jnp.where(spot[0:1] < 0, -1.0, found)

    before = lax.broadcasted_iota(jnp.int32, (rows, rows), 0) >= lax.broadcasted_iota(
        jnp.int32, (rows, rows), 1
    )
    sums = jnp.where((req_col == requests_at(0, rows)) & before, 1.0, 0.0).astype(BF16)
    slot_ids = lax.broadcasted_iota(jnp.int32, (cols_in.shape[0], prior.shape[0]), 1)
    pick_x = jnp.where(slot_ids == cols_in[:, 0:1], 1.0, 0.0).astype(BF16)
    pick_bc = jnp.where(slot_ids == cols_in[:, 0:1] + 6, 1.0, 0.0).astype(BF16)
    spot_ids = lax.broadcasted_iota(jnp.int32, (rows, cols_in.shape[0]), 1).astype(F32)
    chosen = [
        jnp.where((spot_ids == 3 * req_col + offset + (3 - lag)) & (offset < lag), 1.0, 0.0).astype(BF16)
        for lag in (1, 2, 3)
    ]
    xs[0:TILE, :] = jnp.zeros((TILE, x_cols), BF16)
    bs[0:TILE, :] = jnp.zeros((TILE, 128), BF16)
    run[0:TILE, :] = jnp.zeros((TILE, 128), F32)
    step[0:TILE, :] = jnp.zeros((TILE, 128), F32)
    c_ref[rows:, :] = jnp.zeros((c_ref.shape[0] - rows, 128), F32)

    def convolved(here, inputs):
        total = taps[3:4, here] * raw[8:, here]
        for lag in (1, 2, 3):
            shifted = raw[8 - lag : 8 - lag + rows, here]
            value = jnp.where(offset < lag, 0.0, shifted) + dot(chosen[lag - 1], inputs)
            total = total + taps[3 - lag : 4 - lag, here] * value
        return (total / (1.0 + jnp.exp(-total))).astype(BF16)

    for copy in now:
        copy.wait()
    put(raw, 8, slice(x_cols, cols), dot(tok[...], w_bc[...]).astype(BF16), (-3, 3, 4))
    put(step, TILE, slice(None), dot_t(tok[...], w_dt[...]).astype(BF16), (-3, 3, 4))
    out = convolved(slice(x_cols, cols), dot(pick_bc, prior[:, 0 : cols - x_cols]).astype(BF16))
    inputs = dot(pick_x, prior[...]).astype(BF16)
    bs[TILE:, :] = out[:, 0:128]
    cs[...] = out[:, 128:256]
    c_ref[0:rows, :] = out[:, 128:256].astype(F32)
    steps = jax.nn.softplus(step[TILE:, :] + bias[...])
    step[TILE:, :] = steps
    log_keep = -steps * decay[...]
    high = log_keep.astype(BF16)
    left = log_keep - high.astype(F32)
    middle = left.astype(BF16)
    low = (left - middle.astype(F32)).astype(BF16)
    running = dot(sums, high) + dot(sums, middle) + dot(sums, low)
    run[TILE:, :] = running
    fade_ref[0:rows, :] = jnp.exp(running)

    for k, copy in enumerate(chunks):
        copy.wait()
        here = slice(WIDE * k, WIDE * (k + 1))
        put(raw, 8, here, dot(tok[...], w_x[:, here]).astype(BF16), (-3, 3, 4))
        for at in range(WIDE * k, WIDE * (k + 1), 256):
            xs[TILE:, at : at + 256] = convolved(slice(at, at + 256), inputs[:, at : at + 256])

    lanes = lax.broadcasted_iota(jnp.int32, (TILE, 2 * TILE), 1)
    subs = lax.broadcasted_iota(jnp.int32, (TILE, 2 * TILE), 0)
    left = lax.broadcasted_iota(jnp.int32, (2 * TILE, 128), 1) < 64

    def tile(j, carry):
        at = pl.multiple_of(j * TILE, TILE)
        score = dot_t(cs[pl.ds(at, TILE), :], bs[pl.ds(at, 2 * TILE), :])
        around = requests_at(at - TILE, 2 * TILE)
        own = around.reshape(1, 2 * TILE)
        own_col = jnp.sum(
            jnp.where(at + subs >= info[0:1, :], 1.0, 0.0), axis=1, keepdims=True
        )
        mask = (own_col == own) & (lanes - TILE <= subs)
        run_w = run[pl.ds(at, 2 * TILE), :]
        run_rows = run_w.T
        step_rows = step[pl.ds(at, 2 * TILE), :].T
        run_cols = run_w[TILE:, :]
        for pair in range(x_cols // 128):
            mixes = []
            for h in (2 * pair, 2 * pair + 1):
                gap = run_cols[:, h : h + 1] - run_rows[h : h + 1, :]
                mix = jnp.exp(jnp.where(mask, gap, -jnp.inf)) * score * step_rows[h : h + 1, :]
                mixes.append(mix.astype(BF16))
            here = slice(128 * pair, 128 * (pair + 1))
            x_w = xs[pl.ds(at, 2 * TILE), here]
            nothing = jnp.zeros_like(x_w)
            both = jnp.concatenate([jnp.where(left, x_w, nothing), jnp.where(left, nothing, x_w)], axis=0)
            out = dot(jnp.concatenate(mixes, axis=1), both)
            sum_ref[pair, pl.ds(at, TILE), :] = out + skip[:, here] * x_w[TILE:].astype(F32)
        return carry

    lax.fori_loop(0, rows // TILE, tile, 0)
    sum_ref[:, rows:, :] = jnp.zeros((x_cols // 128, sum_ref.shape[1] - rows, 128), F32)
    fade_ref[rows:, :] = jnp.zeros((fade_ref.shape[0] - rows, 128), F32)
    add_carried(table, 0, parts, c_ref, fade_ref, states, sum_ref, state_sem)


def fetch_states(table, first, arrays, states, sems):
    state_size = states.shape[1]
    for k, array in enumerate(arrays):

        def begin(i, carry, array=array):
            at = pl.multiple_of(table[2, i] * state_size, state_size)
            pltpu.make_async_copy(array.at[pl.ds(at, state_size), :], states.at[i], sems.at[i]).start()
            return carry

        lax.fori_loop(table[3, first + k], table[3, first + k + 1], begin, 0)


def add_carried(table, first, arrays, c_ref, fade_ref, states, total, sems):
    requests, state_size, x_cols = states.shape
    begins, ends = table[3, first], table[3, first + len(arrays)]
    row = lax.broadcasted_iota(jnp.int32, (32, 128), 0)
    lane_head = lax.broadcasted_iota(jnp.int32, (128, x_cols), 1) // 64
    spread = jnp.where(lane_head == lax.broadcasted_iota(jnp.int32, (128, x_cols), 0), 1.0, 0.0).astype(BF16)
    side = 4

    def some(group, carry):
        picks = []
        for k in range(side):
            i = begins + group * side + k

            @pl.when(i < ends)
            def _():
                pltpu.make_async_copy(
                    arrays[0].at[pl.ds(0, state_size), :], states.at[i], sems.at[i]
                ).wait()

            safe = jnp.minimum(i, requests - 1)
            picks.append((safe, table[0, safe], jnp.where(i < ends, table[1, safe], 0)))
        terms = []
        for i, start, _ in picks:
            fade = fade_ref[pl.ds(start, 32), :]
            high = fade.astype(BF16)
            low = (fade - high.astype(F32)).astype(BF16)
            scale = dot(jnp.concatenate([high, low], axis=0), spread)
            product = dot(c_ref[pl.ds(start, 32), :].astype(BF16), states[i])
            terms.append((scale[0:32] + scale[32:64]) * product)
        for term, (_, start, length) in zip(terms, picks):
            inside = row < length
            for k in range(x_cols // 128):
                old = total[k, pl.ds(start, 32), :]
                total[k, pl.ds(start, 32), :] = jnp.where(
                    inside, old + term[:, 128 * k : 128 * (k + 1)], old
                )
        return carry

    lax.fori_loop(0, lax.div(ends - begins + side - 1, side), some, 0)


def late_kernel(first, count, table, *refs):
    arrays, (c_ref, fade_ref, before, out, states, total, sems, got) = refs[:count], refs[count:]
    rows = out.shape[0]
    copy = pltpu.make_async_copy(before, total, got)
    copy.start()
    fetch_states(table, first, arrays, states, sems)
    copy.wait()
    add_carried(table, first, arrays, c_ref, fade_ref, states, total, sems)
    for k in range(total.shape[0]):
        out[:, 128 * k : 128 * (k + 1)] = total[k, 0:rows, :].astype(BF16)


VMEM = pl.BlockSpec(memory_space=pltpu.VMEM)
SMEM = pl.BlockSpec(memory_space=pltpu.SMEM)
HBM = pl.BlockSpec(memory_space=pltpu.HBM)


def weight_scratch(weights, rows, copies):
    depth, x_cols = weights[0].shape
    return [
        pltpu.VMEM((rows, depth), BF16),
        pltpu.VMEM((depth, x_cols), BF16),
        pltpu.VMEM((depth, weights[1].shape[1]), BF16),
        pltpu.VMEM((128, depth), BF16),
        pltpu.SemaphoreType.DMA((copies + 2 + x_cols // WIDE,)),
    ]


def project(blocks, weights):
    rows, x_cols = sum(b.shape[0] for b in blocks), weights[0].shape[1]
    return pl.pallas_call(
        project_kernel,
        out_shape=(
            jax.ShapeDtypeStruct((rows, x_cols), BF16),
            jax.ShapeDtypeStruct((rows, weights[1].shape[1] + 128), BF16),
        ),
        in_specs=[HBM] * (len(blocks) + 3),
        out_specs=(VMEM, VMEM),
        scratch_shapes=weight_scratch(weights, rows, len(blocks)),
        compiler_params=pltpu.CompilerParams(vmem_limit_bytes=MOST),
        cost_estimate=pl.CostEstimate(flops=8000000000, bytes_accessed=14000000, transcendentals=0),
        name="project",
    )(*blocks, *weights)


def mixer_inner(z, table, blocks, weights, parts, priors, projected, info, columns, taps, bias, decay, skip):
    block_rows = blocks[0].shape[0]
    rows, x_cols, cols = NZ * block_rows, weights[0].shape[1], taps.shape[1]
    requests, state_size, margin = table.shape[1] - 1, 128, 32
    return pl.pallas_call(
        inner_kernel,
        out_shape=(
            jax.ShapeDtypeStruct((x_cols // 128, rows + margin, 128), F32),
            jax.ShapeDtypeStruct((rows + margin, 128), F32),
            jax.ShapeDtypeStruct((rows + margin, 128), F32),
        ),
        in_specs=[SMEM] * 2 + [HBM] * 13 + [VMEM] * 8,
        out_specs=(VMEM, VMEM, VMEM),
        scratch_shapes=[
            pltpu.VMEM((rows + 8, cols), F32),
            pltpu.VMEM((rows + TILE, x_cols), BF16),
            pltpu.VMEM((rows + TILE, 128), BF16),
            pltpu.VMEM((rows, 128), BF16),
            pltpu.VMEM((rows + TILE, 128), F32),
            pltpu.VMEM((rows + TILE, 128), F32),
        ]
        + weight_scratch(weights, 3 * block_rows, len(blocks))
        + [
            pltpu.VMEM((requests, state_size, x_cols), BF16),
            pltpu.SemaphoreType.DMA((requests,)),
            pltpu.VMEM((8 * PRIORS, x_cols), BF16),
            pltpu.SemaphoreType.DMA((2,)),
        ],
        compiler_params=pltpu.CompilerParams(vmem_limit_bytes=MOST),
        cost_estimate=pl.CostEstimate(flops=16000000000, bytes_accessed=18000000, transcendentals=2000000),
        name="mixer_inner",
    )(z, table, *blocks, *weights, *parts, *priors, *projected, info, columns, taps, bias, decay, skip)


def mixer_late(table, first, arrays, c_rows, fade, total, rows):
    x_cols = total.shape[0] * 128
    state_size, requests = c_rows.shape[1], table.shape[1] - 1
    return pl.pallas_call(
        lambda *refs: late_kernel(first, len(arrays), *refs),
        out_shape=jax.ShapeDtypeStruct((rows, x_cols), BF16),
        in_specs=[SMEM] + [HBM] * len(arrays) + [VMEM] * 2 + [HBM],
        out_specs=VMEM,
        scratch_shapes=[
            pltpu.VMEM((requests, state_size, x_cols), BF16),
            pltpu.VMEM(total.shape, F32),
            pltpu.SemaphoreType.DMA((requests,)),
            pltpu.SemaphoreType.DMA,
        ],
        compiler_params=pltpu.CompilerParams(vmem_limit_bytes=MOST),
        cost_estimate=pl.CostEstimate(flops=500000000, bytes_accessed=13000000, transcendentals=0),
        name="mixer_late",
    )(table, *arrays, c_rows, fade, total)


def shards(
    tokens, weight_x, weight_bc, weight_dt, kernel_x, kernel_bc, dt_bias, decay_rate, skip_gain,
    ssm_pool, conv_x_pool, conv_bc_pool, hit_holder, hit_slot, suffix_len,
):
    model_dim, heads = weight_dt.shape
    x_cols = weight_x.shape[1]
    bc_cols = weight_bc.shape[1] * weight_bc.shape[2]
    slots, head_size, state_size = ssm_pool.shape[0], ssm_pool.shape[2], ssm_pool.shape[3]
    requests = suffix_len.shape[1]
    me, z = lax.axis_index("cache"), lax.axis_index("tp")

    weights = (weight_x, weight_bc.reshape(model_dim, bc_cols), weight_dt.T)

    lengths = suffix_len[0]
    order = jnp.arange(requests, dtype=jnp.int32)
    ends = jnp.sum(jnp.where(order[None, :] <= order[:, None], lengths[None, :], 0), axis=1)
    starts = ends - lengths
    holder = lax.dynamic_slice_in_dim(hit_holder[:, 0], me * requests, requests)
    slot = lax.dynamic_slice_in_dim(hit_slot, me * requests, requests)
    my_y, my_x, my_c = me // (2 * NX), (me // 2) % NX, me % 2
    at_y, at_x, at_c = holder // (2 * NX), (holder // 2) % NX, holder % 2
    far_y, far_x = (my_y - at_y) % NY, (my_x - at_x) % NX
    outer, inner = jnp.where(at_c == 0, far_y, far_x), jnp.where(at_c == 0, far_x, far_y)
    node = jnp.where(inner == 2, 3, jnp.where(inner == 3, 2, inner))
    line = jnp.where(outer == 2, 3, jnp.where(outer == 3, 2, outer))
    prior_row = ((at_c != my_c) * NY + line) * PRIORS + node * PRIOR + slot * 3
    block = 2 * node + slot
    part_of = jnp.where(outer == 2, 3 + block // 4, line)
    block = jnp.where(outer == 2, block % 4, block)
    own = at_c == my_c
    array = jnp.where(
        part_of < 3,
        jnp.where(part_of == 0, jnp.where(own, 0, 1), jnp.where(own, 1, 3) + part_of),
        jnp.where(own, 0, 1) + 2 * part_of,
    )
    key = array * requests + order
    rank = jnp.sum((key[None, :] < key[:, None]).astype(jnp.int32), axis=1)
    sorting = (rank[None, :] == order[:, None]).astype(jnp.int32)
    by_array = jnp.sum(sorting[None] * jnp.stack([starts, lengths, block])[:, None, :], axis=2)
    firsts = jnp.sum((array[None, :] < order[:, None]).astype(jnp.int32), axis=1)
    table = jnp.concatenate([by_array, firsts[None]], axis=0).astype(jnp.int32)
    table = jnp.pad(table, ((0, 0), (0, 1)))
    info = jnp.stack([ends, starts])
    info = jnp.concatenate([info, jnp.full((2, 128 - requests), 1 << 20, jnp.int32)], axis=1)

    taps = jnp.concatenate([kernel_x, kernel_bc.reshape(4, bc_cols)], axis=1).astype(F32)
    pad = (0, 128 - heads)
    from_row = (prior_row[:, None] + jnp.arange(3)[None, :]).reshape(-1)
    from_row = jnp.pad(from_row, (0, 128 - 3 * requests), constant_values=-16)
    columns = jnp.stack([from_row, info[0]], axis=1)
    tables = (
        table, weights, info, columns, taps, jnp.pad(dt_bias, pad)[None], jnp.pad(decay_rate, pad)[None],
        jnp.repeat(skip_gain, head_size)[None],
    )

    def inner(blocks, projected, parts, priors, tables):
        table, weights, info, columns, taps, bias, decay, skip = tables
        sums = mixer_inner(
            z.reshape(1), table, blocks, weights, parts, priors, projected, info, columns, taps,
            bias, decay, skip,
        )
        return sums, table

    states = jnp.swapaxes(ssm_pool.reshape(slots, heads * head_size, state_size), 1, 2)
    conv_bc = jnp.pad(conv_bc_pool.reshape(slots * 3, bc_cols), ((0, PRIOR - 12), (0, x_cols - bc_cols)))
    pool = jnp.concatenate(
        [states.reshape(slots * state_size, x_cols), conv_x_pool.reshape(slots * 3, x_cols), conv_bc]
    )
    late, ((total, c_rows, fade), table) = gather(pool, tokens, tables, project, inner)
    return mixer_late(table, 4, late, c_rows, fade, total, NZ * tokens.shape[0])


def solution(mesh):
    in_specs = (
        P(("cache", "tp"), None), P(None, "tp"), P(None, None, "tp"), P(None, "tp"), P(None, "tp"),
        P(None, None, "tp"), P("tp"), P("tp"), P("tp"), P("cache", "tp", None, None), P("cache", None, "tp"),
        P("cache", None, None, "tp"), P(), P(), P("cache", None),
    )
    return jax.shard_map(
        shards, mesh=mesh, in_specs=in_specs, out_specs=P("cache", "tp"), check_vma=False
    )
```

```python
import jax
import jax.numpy as jnp
from jax import lax
from jax.experimental import pallas as pl
from jax.experimental.pallas import tpu as pltpu
from jax.sharding import PartitionSpec as P

NX, NY, NZ = 4, 4, 8
MOST = 60 * 1024 * 1024
TILE = 64
PRIOR = 16
PRIORS = NX * PRIOR
WIDE = 512
F32, BF16 = jnp.float32, jnp.bfloat16


def chip(y, x, c):
    return (y % NY) * 2 * NX + (x % NX) * 2 + c


def every():
    return [(y, x, c) for y in range(NY) for x in range(NX) for c in range(2)]


def first_round(step):
    return [(chip(y, x, c), chip(y + c * step, x + (1 - c) * step, c)) for y, x, c in every()]


def second_round(step):
    return [(chip(y, x, c), chip(y + (1 - c) * step, x + c * step, c)) for y, x, c in every()]


CORES = [(chip(y, x, c), chip(y, x, 1 - c)) for y, x, c in every()]


def over_z(value, step):
    return lax.ppermute(value, "tp", [(z, (z + step) % NZ) for z in range(NZ)])


def on_cache(value, pairs):
    return lax.ppermute(value, "cache", pairs)


def moved(name, sources, shapes, moves):
    def kernel(*refs):
        ins, (outs, held, sems) = refs[: len(sources)], (refs[len(sources) : -2], refs[-2], refs[-1])
        inward, outward, first = [], [], 0
        for k, (src, at, count, dst, to) in enumerate(moves):
            spot = held.at[pl.ds(first, count), :]
            inward.append(pltpu.make_async_copy(ins[src].at[pl.ds(at, count), :], spot, sems.at[2 * k]))
            outward.append(pltpu.make_async_copy(spot, outs[dst].at[pl.ds(to, count), :], sems.at[2 * k + 1]))
            first += count
        for copy in inward:
            copy.start()
        for before, after in zip(inward, outward):
            before.wait()
            after.start()
        for copy in outward:
            copy.wait()

    rows = sum(move[2] for move in moves)
    return pl.pallas_call(
        kernel,
        out_shape=[jax.ShapeDtypeStruct(shape, sources[0].dtype) for shape in shapes],
        in_specs=[pl.BlockSpec(memory_space=pltpu.HBM)] * len(sources),
        out_specs=[pl.BlockSpec(memory_space=pltpu.HBM)] * len(shapes),
        scratch_shapes=[
            pltpu.VMEM((rows, sources[0].shape[1]), sources[0].dtype),
            pltpu.SemaphoreType.DMA((2 * len(moves),)),
        ],
        compiler_params=pltpu.CompilerParams(vmem_limit_bytes=MOST),
        cost_estimate=pl.CostEstimate(flops=0, bytes_accessed=4000000, transcendentals=0),
        name=name,
    )(*sources)


def lined(nodes):
    states, cols = nodes[0].shape[0] - PRIOR, nodes[0].shape[1]
    moves = []
    for k in range(len(nodes)):
        moves.append((k, 0, states, 0, k * states))
        moves.append((k, states, PRIOR, 0, len(nodes) * states + k * PRIOR))
        moves.append((k, states, PRIOR, 1, k * PRIOR))
    shapes = [(len(nodes) * (states + PRIOR), cols), (len(nodes) * PRIOR, cols)]
    return moved("lined", nodes, shapes, moves)


def gathered_priors(lines):
    moves = [(k, line.shape[0] - PRIORS, PRIORS, 0, k * PRIORS) for k, line in enumerate(lines)]
    return moved("gathered_priors", lines, [(len(lines) * PRIORS, lines[0].shape[1])], moves)[0]


def halves(top, bottom, spare=0):
    rows, cols = (top.shape[0] - spare) // 2, top.shape[1]
    return moved("halves", [top, bottom], [(rows, cols)] * 2, [(0, 0, rows, 0, 0), (1, rows, rows, 1, 0)])


def gather(pool, tokens, tables, project, inner):
    tie = lax.optimization_barrier
    near_up, near_down = on_cache(pool, first_round(1)), on_cache(pool, first_round(-1))
    far = on_cache(pool, first_round(2))
    up, down = over_z(tokens, 1), over_z(tokens, -1)
    blocks = [tokens, up, down]
    up, down = over_z(up, 1), over_z(down, -1)
    blocks += [up, down]
    near_up, near_down, far, tables = tie((near_up, near_down, far, tables))
    line, line_prior = lined([pool, near_up, near_down, far])
    line, line_prior, up, down, blocks = tie((line, line_prior, up, down, blocks))

    near_up, near_down = on_cache(line, second_round(1)), on_cache(line, second_round(-1))
    far_prior = on_cache(line_prior, second_round(2))
    line_other = on_cache(line, CORES)
    projected = [project(blocks, tables[1])]
    up, down = over_z(up, 1), over_z(down, -1)
    up, down, projected = tie((up, down, projected))
    last_up, last_down = halves(up, down)
    blocks = [up, down, over_z(last_up, 1), over_z(last_down, -1)]
    blocks, line_other = tie((blocks, line_other))
    projected.append(project(blocks, tables[1]))
    near_up, near_down, far_prior, projected = tie((near_up, near_down, far_prior, projected))

    priors = gathered_priors([line_prior, near_up, near_down, far_prior])
    priors = [priors, on_cache(priors, CORES)]
    far_up, far_down = halves(near_up, near_down, PRIORS)
    far_up, far_down = on_cache(far_up, second_round(1)), on_cache(far_down, second_round(-1))
    up_other, down_other = on_cache(near_up, CORES), on_cache(near_down, CORES)
    result = inner(projected, [line, line_other, near_up, near_down], priors, tables)
    far_up, far_down, result = tie((far_up, far_down, result))
    far_others = [on_cache(far_up, CORES), on_cache(far_down, CORES)]
    return [up_other, down_other, far_up, far_others[0], far_down, far_others[1]], result


def dot(a, b):
    return jnp.dot(a, b, preferred_element_type=F32)


def dot_t(a, b):
    return lax.dot_general(a, b, (((1,), (1,)), ((), ())), preferred_element_type=F32)


def fetched(blocks, weights, tok, held, sem):
    w_x_in, w_bc_in, w_dt_in = weights
    w_x, w_bc, w_dt = held
    now, at = [], 0
    for block in blocks:
        now.append(pltpu.make_async_copy(block, tok.at[pl.ds(at, block.shape[0]), :], sem.at[len(now)]))
        at += block.shape[0]
    heads = w_dt_in.shape[0]
    now.append(pltpu.make_async_copy(w_bc_in, w_bc, sem.at[len(now)]))
    now.append(pltpu.make_async_copy(w_dt_in, w_dt.at[pl.ds(0, heads), :], sem.at[len(now)]))
    chunks = []
    for k in range(w_x.shape[1] // WIDE):
        here = (slice(None), slice(WIDE * k, WIDE * (k + 1)))
        chunks.append(pltpu.make_async_copy(w_x_in.at[here], w_x.at[here], sem.at[len(now) + k]))
    for copy in now + chunks:
        copy.start()
    w_dt[heads:, :] = jnp.zeros((128 - heads, w_dt.shape[1]), BF16)
    return now, chunks


def project_kernel(*refs):
    blocks, (w_x_in, w_bc_in, w_dt_in, x_out, b_out, tok, w_x, w_bc, w_dt, sem) = refs[:-10], refs[-10:]
    now, chunks = fetched(blocks, (w_x_in, w_bc_in, w_dt_in), tok, (w_x, w_bc, w_dt), sem)
    for copy in now:
        copy.wait()
    b_out[:, 0:256] = dot(tok[...], w_bc[...]).astype(BF16)
    b_out[:, 256:384] = dot_t(tok[...], w_dt[...]).astype(BF16)
    for k, copy in enumerate(chunks):
        copy.wait()
        here = slice(WIDE * k, WIDE * (k + 1))
        x_out[:, here] = dot(tok[...], w_x[:, here]).astype(BF16)


def inner_kernel(
    where, table, s0, s1, s2, s3, p0, p1, x_first, b_first, x_next, b_next, info, cols_in, taps, bias, decay, skip, sum_ref,
    raw, xs, bs, cs, run, step, states, state_sem, prior, prior_sem,
):
    rows = raw.shape[0] - 8
    x_cols = xs.shape[1]
    c_ref, fade_ref = sum_ref.at[x_cols // 128], sum_ref.at[x_cols // 128 + 1]
    cols = taps.shape[1]
    block = rows // NZ
    z = where[0]
    now = []
    parts = (s0, s1, s2, s3)
    fetch_states(table, 0, parts, states, state_sem)
    for k, source in enumerate((p0, p1)):
        spot = prior.at[pl.ds(k * p0.shape[0], p0.shape[0]), :]
        now.append(pltpu.make_async_copy(source, spot, prior_sem.at[k]))
        now[-1].start()

    def put(target, lead, columns, values, shifts):
        for k, shift in enumerate(shifts):
            at = pl.multiple_of(lax.rem(z + shift + NZ, NZ) * block, block)
            target[pl.ds(lead + at, block), columns] = values[k * block : (k + 1) * block].astype(F32)

    put(raw, 8, slice(0, x_cols), x_first, (0, -1, 1, -2, 2))
    put(raw, 8, slice(x_cols, cols), b_first[:, 0:256], (0, -1, 1, -2, 2))
    put(step, TILE, slice(None), b_first[:, 256:384], (0, -1, 1, -2, 2))
    put(raw, 8, slice(0, x_cols), x_next, (-3, 3, 4))
    put(raw, 8, slice(x_cols, cols), b_next[:, 0:256], (-3, 3, 4))
    put(step, TILE, slice(None), b_next[:, 256:384], (-3, 3, 4))
    raw[0:8, :] = jnp.zeros((8, cols), F32)

    position = lax.broadcasted_iota(jnp.int32, (rows, 128), 0)
    request = lax.broadcasted_iota(jnp.int32, (rows, 128), 1).astype(F32)
    req_col = jnp.sum(jnp.where(position >= info[0:1, :], 1.0, 0.0), axis=1, keepdims=True)
    is_own = request == req_col
    own_start = jnp.sum(jnp.where(is_own, info[1:2, :].astype(F32), 0.0), axis=1, keepdims=True)
    offset = position[:, 0:1].astype(F32) - own_start

    def requests_at(first, count):
        spot = first + lax.broadcasted_iota(jnp.int32, (info.shape[1], count), 1)
        found = jnp.sum(jnp.where(spot >= cols_in[:, 1:2], 1.0, 0.0), axis=0, keepdims=True)
        return jnp.where(spot[0:1] < 0, -1.0, found)

    before = lax.broadcasted_iota(jnp.int32, (rows, rows), 0) >= lax.broadcasted_iota(
        jnp.int32, (rows, rows), 1
    )
    sums = jnp.where((req_col == requests_at(0, rows)) & before, 1.0, 0.0).astype(BF16)
    slot_ids = lax.broadcasted_iota(jnp.int32, (cols_in.shape[0], prior.shape[0]), 1)
    pick_x = jnp.where(slot_ids == cols_in[:, 0:1], 1.0, 0.0).astype(BF16)
    pick_bc = jnp.where(slot_ids == cols_in[:, 0:1] + 6, 1.0, 0.0).astype(BF16)
    spot_ids = lax.broadcasted_iota(jnp.int32, (rows, cols_in.shape[0]), 1).astype(F32)
    chosen = [
        jnp.where((spot_ids == 3 * req_col + offset + (3 - lag)) & (offset < lag), 1.0, 0.0).astype(BF16)
        for lag in (1, 2, 3)
    ]
    xs[0:TILE, :] = jnp.zeros((TILE, x_cols), BF16)
    bs[0:TILE, :] = jnp.zeros((TILE, 128), BF16)
    run[0:TILE, :] = jnp.zeros((TILE, 128), F32)
    step[0:TILE, :] = jnp.zeros((TILE, 128), F32)
    c_ref[rows:, :] = jnp.zeros((c_ref.shape[0] - rows, 128), F32)

    def convolved(here, inputs):
        total = taps[3:4, here] * raw[8:, here]
        for lag in (1, 2, 3):
            shifted = raw[8 - lag : 8 - lag + rows, here]
            value = jnp.where(offset < lag, 0.0, shifted) + dot(chosen[lag - 1], inputs)
            total = total + taps[3 - lag : 4 - lag, here] * value
        return (total / (1.0 + jnp.exp(-total))).astype(BF16)

    for copy in now:
        copy.wait()
    out = convolved(slice(x_cols, cols), dot(pick_bc, prior[:, 0 : cols - x_cols]).astype(BF16))
    inputs = dot(pick_x, prior[...]).astype(BF16)
    bs[TILE:, :] = out[:, 0:128]
    cs[...] = out[:, 128:256]
    c_ref[0:rows, :] = out[:, 128:256].astype(F32)
    steps = jax.nn.softplus(step[TILE:, :] + bias[...])
    step[TILE:, :] = steps
    log_keep = -steps * decay[...]
    high = log_keep.astype(BF16)
    left = log_keep - high.astype(F32)
    middle = left.astype(BF16)
    low = (left - middle.astype(F32)).astype(BF16)
    running = dot(sums, high) + dot(sums, middle) + dot(sums, low)
    run[TILE:, :] = running
    fade_ref[0:rows, :] = jnp.exp(running)

    for at in range(0, x_cols, 256):
        xs[TILE:, at : at + 256] = convolved(slice(at, at + 256), inputs[:, at : at + 256])

    lanes = lax.broadcasted_iota(jnp.int32, (TILE, 2 * TILE), 1)
    subs = lax.broadcasted_iota(jnp.int32, (TILE, 2 * TILE), 0)
    left = lax.broadcasted_iota(jnp.int32, (2 * TILE, 128), 1) < 64

    def tile(j, carry):
        at = pl.multiple_of(j * TILE, TILE)
        score = dot_t(cs[pl.ds(at, TILE), :], bs[pl.ds(at, 2 * TILE), :])
        around = requests_at(at - TILE, 2 * TILE)
        own = around.reshape(1, 2 * TILE)
        own_col = jnp.sum(
            jnp.where(at + subs >= info[0:1, :], 1.0, 0.0), axis=1, keepdims=True
        )
        mask = (own_col == own) & (lanes - TILE <= subs)
        run_w = run[pl.ds(at, 2 * TILE), :]
        run_rows = run_w.T
        step_rows = step[pl.ds(at, 2 * TILE), :].T
        run_cols = run_w[TILE:, :]
        for pair in range(x_cols // 128):
            mixes = []
            for h in (2 * pair, 2 * pair + 1):
                gap = run_cols[:, h : h + 1] - run_rows[h : h + 1, :]
                mix = jnp.exp(jnp.where(mask, gap, -jnp.inf)) * score * step_rows[h : h + 1, :]
                mixes.append(mix.astype(BF16))
            here = slice(128 * pair, 128 * (pair + 1))
            x_w = xs[pl.ds(at, 2 * TILE), here]
            nothing = jnp.zeros_like(x_w)
            both = jnp.concatenate([jnp.where(left, x_w, nothing), jnp.where(left, nothing, x_w)], axis=0)
            out = dot(jnp.concatenate(mixes, axis=1), both)
            sum_ref[pair, pl.ds(at, TILE), :] = out + skip[:, here] * x_w[TILE:].astype(F32)
        return carry

    lax.fori_loop(0, rows // TILE, tile, 0)
    sum_ref[0 : x_cols // 128, rows:, :] = jnp.zeros((x_cols // 128, sum_ref.shape[1] - rows, 128), F32)
    fade_ref[rows:, :] = jnp.zeros((fade_ref.shape[0] - rows, 128), F32)
    add_carried(table, 0, parts, c_ref, fade_ref, states, sum_ref, state_sem)


def fetch_states(table, first, arrays, states, sems):
    state_size = states.shape[1]
    for k, array in enumerate(arrays):

        def begin(i, carry, array=array):
            at = pl.multiple_of(table[2, i] * state_size, state_size)
            pltpu.make_async_copy(array.at[pl.ds(at, state_size), :], states.at[i], sems.at[i]).start()
            return carry

        lax.fori_loop(table[3, first + k], table[3, first + k + 1], begin, 0)


def add_carried(table, first, arrays, c_ref, fade_ref, states, total, sems):
    requests, state_size, x_cols = states.shape
    begins, ends = table[3, first], table[3, first + len(arrays)]
    row = lax.broadcasted_iota(jnp.int32, (32, 128), 0)
    lane_head = lax.broadcasted_iota(jnp.int32, (128, x_cols), 1) // 64
    spread = jnp.where(lane_head == lax.broadcasted_iota(jnp.int32, (128, x_cols), 0), 1.0, 0.0).astype(BF16)
    side = 4

    def some(group, carry):
        picks = []
        for k in range(side):
            i = begins + group * side + k

            @pl.when(i < ends)
            def _():
                pltpu.make_async_copy(
                    arrays[0].at[pl.ds(0, state_size), :], states.at[i], sems.at[i]
                ).wait()

            safe = jnp.minimum(i, requests - 1)
            picks.append((safe, table[0, safe], jnp.where(i < ends, table[1, safe], 0)))
        terms = []
        for i, start, _ in picks:
            fade = fade_ref[pl.ds(start, 32), :]
            high = fade.astype(BF16)
            low = (fade - high.astype(F32)).astype(BF16)
            scale = dot(jnp.concatenate([high, low], axis=0), spread)
            product = dot(c_ref[pl.ds(start, 32), :].astype(BF16), states[i])
            terms.append((scale[0:32] + scale[32:64]) * product)
        for term, (_, start, length) in zip(terms, picks):
            inside = row < length
            for k in range(x_cols // 128):
                old = total[k, pl.ds(start, 32), :]
                total[k, pl.ds(start, 32), :] = jnp.where(
                    inside, old + term[:, 128 * k : 128 * (k + 1)], old
                )
        return carry

    lax.fori_loop(0, lax.div(ends - begins + side - 1, side), some, 0)


def late_kernel(first, count, table, *refs):
    arrays, (before, out, states, total, sems, got) = refs[:count], refs[count:]
    rows, x_cols = out.shape
    c_ref, fade_ref = total.at[x_cols // 128], total.at[x_cols // 128 + 1]
    copy = pltpu.make_async_copy(before, total, got)
    copy.start()
    fetch_states(table, first, arrays, states, sems)
    copy.wait()
    add_carried(table, first, arrays, c_ref, fade_ref, states, total, sems)
    for k in range(x_cols // 128):
        out[:, 128 * k : 128 * (k + 1)] = total[k, 0:rows, :].astype(BF16)


VMEM = pl.BlockSpec(memory_space=pltpu.VMEM)
SMEM = pl.BlockSpec(memory_space=pltpu.SMEM)
HBM = pl.BlockSpec(memory_space=pltpu.HBM)
ANY = pl.BlockSpec(memory_space=pl.ANY)


def weight_scratch(weights, rows, copies):
    depth, x_cols = weights[0].shape
    return [
        pltpu.VMEM((rows, depth), BF16),
        pltpu.VMEM((depth, x_cols), BF16),
        pltpu.VMEM((depth, weights[1].shape[1]), BF16),
        pltpu.VMEM((128, depth), BF16),
        pltpu.SemaphoreType.DMA((copies + 2 + x_cols // WIDE,)),
    ]


def project(blocks, weights):
    rows, x_cols = sum(b.shape[0] for b in blocks), weights[0].shape[1]
    return pl.pallas_call(
        project_kernel,
        out_shape=(
            jax.ShapeDtypeStruct((rows, x_cols), BF16),
            jax.ShapeDtypeStruct((rows, weights[1].shape[1] + 128), BF16),
        ),
        in_specs=[HBM] * (len(blocks) + 3),
        out_specs=(VMEM, VMEM),
        scratch_shapes=weight_scratch(weights, rows, len(blocks)),
        compiler_params=pltpu.CompilerParams(vmem_limit_bytes=MOST),
        cost_estimate=pl.CostEstimate(flops=8000000000, bytes_accessed=14000000, transcendentals=0),
        name="project",
    )(*blocks, *weights)


def mixer_inner(z, table, parts, priors, projected, info, columns, taps, bias, decay, skip):
    rows = sum(p[0].shape[0] for p in projected)
    x_cols, cols = projected[0][0].shape[1], taps.shape[1]
    requests, state_size, margin = table.shape[1] - 1, 128, 32
    return pl.pallas_call(
        inner_kernel,
        out_shape=jax.ShapeDtypeStruct((x_cols // 128 + 2, rows + margin, 128), F32),
        in_specs=[SMEM] * 2 + [HBM] * 6 + [VMEM] * 10,
        out_specs=VMEM,
        scratch_shapes=[
            pltpu.VMEM((rows + 8, cols), F32),
            pltpu.VMEM((rows + TILE, x_cols), BF16),
            pltpu.VMEM((rows + TILE, 128), BF16),
            pltpu.VMEM((rows, 128), BF16),
            pltpu.VMEM((rows + TILE, 128), F32),
            pltpu.VMEM((rows + TILE, 128), F32),
            pltpu.VMEM((requests, state_size, x_cols), BF16),
            pltpu.SemaphoreType.DMA((requests,)),
            pltpu.VMEM((8 * PRIORS, x_cols), BF16),
            pltpu.SemaphoreType.DMA((2,)),
        ],
        compiler_params=pltpu.CompilerParams(vmem_limit_bytes=MOST),
        cost_estimate=pl.CostEstimate(flops=14000000000, bytes_accessed=18000000, transcendentals=2000000),
        name="mixer_inner",
    )(z, table, *parts, *priors, *projected[0], *projected[1], info, columns, taps, bias, decay, skip)


def mixer_late(table, first, arrays, total, rows):
    x_cols = (total.shape[0] - 2) * 128
    state_size, requests = total.shape[2], table.shape[1] - 1
    return pl.pallas_call(
        lambda *refs: late_kernel(first, len(arrays), *refs),
        out_shape=jax.ShapeDtypeStruct((rows, x_cols), BF16),
        in_specs=[SMEM] + [ANY] * (len(arrays) + 1),
        out_specs=VMEM,
        scratch_shapes=[
            pltpu.VMEM((requests, state_size, x_cols), BF16),
            pltpu.VMEM(total.shape, F32),
            pltpu.SemaphoreType.DMA((requests,)),
            pltpu.SemaphoreType.DMA,
        ],
        compiler_params=pltpu.CompilerParams(vmem_limit_bytes=24 * 1024 * 1024),
        cost_estimate=pl.CostEstimate(flops=500000000, bytes_accessed=13000000, transcendentals=0),
        name="mixer_late",
    )(table, *arrays, total)


def shards(
    tokens, weight_x, weight_bc, weight_dt, kernel_x, kernel_bc, dt_bias, decay_rate, skip_gain,
    ssm_pool, conv_x_pool, conv_bc_pool, hit_holder, hit_slot, suffix_len,
):
    model_dim, heads = weight_dt.shape
    x_cols = weight_x.shape[1]
    bc_cols = weight_bc.shape[1] * weight_bc.shape[2]
    slots, head_size, state_size = ssm_pool.shape[0], ssm_pool.shape[2], ssm_pool.shape[3]
    requests = suffix_len.shape[1]
    me, z = lax.axis_index("cache"), lax.axis_index("tp")

    weights = (weight_x, weight_bc.reshape(model_dim, bc_cols), weight_dt.T)

    lengths = suffix_len[0]
    order = jnp.arange(requests, dtype=jnp.int32)
    ends = jnp.sum(jnp.where(order[None, :] <= order[:, None], lengths[None, :], 0), axis=1)
    starts = ends - lengths
    holder = lax.dynamic_slice_in_dim(hit_holder[:, 0], me * requests, requests)
    slot = lax.dynamic_slice_in_dim(hit_slot, me * requests, requests)
    my_y, my_x, my_c = me // (2 * NX), (me // 2) % NX, me % 2
    at_y, at_x, at_c = holder // (2 * NX), (holder // 2) % NX, holder % 2
    far_y, far_x = (my_y - at_y) % NY, (my_x - at_x) % NX
    outer, inner = jnp.where(at_c == 0, far_y, far_x), jnp.where(at_c == 0, far_x, far_y)
    node = jnp.where(inner == 2, 3, jnp.where(inner == 3, 2, inner))
    line = jnp.where(outer == 2, 3, jnp.where(outer == 3, 2, outer))
    prior_row = ((at_c != my_c) * NY + line) * PRIORS + node * PRIOR + slot * 3
    block = 2 * node + slot
    part_of = jnp.where(outer == 2, 3 + block // 4, line)
    block = jnp.where(outer == 2, block % 4, block)
    own = at_c == my_c
    array = jnp.where(
        part_of < 3,
        jnp.where(part_of == 0, jnp.where(own, 0, 1), jnp.where(own, 1, 3) + part_of),
        jnp.where(own, 0, 1) + 2 * part_of,
    )
    key = array * requests + order
    rank = jnp.sum((key[None, :] < key[:, None]).astype(jnp.int32), axis=1)
    sorting = (rank[None, :] == order[:, None]).astype(jnp.int32)
    by_array = jnp.sum(sorting[None] * jnp.stack([starts, lengths, block])[:, None, :], axis=2)
    firsts = jnp.sum((array[None, :] < order[:, None]).astype(jnp.int32), axis=1)
    table = jnp.concatenate([by_array, firsts[None]], axis=0).astype(jnp.int32)
    table = jnp.pad(table, ((0, 0), (0, 1)))
    info = jnp.stack([ends, starts])
    info = jnp.concatenate([info, jnp.full((2, 128 - requests), 1 << 20, jnp.int32)], axis=1)

    taps = jnp.concatenate([kernel_x, kernel_bc.reshape(4, bc_cols)], axis=1).astype(F32)
    pad = (0, 128 - heads)
    from_row = (prior_row[:, None] + jnp.arange(3)[None, :]).reshape(-1)
    from_row = jnp.pad(from_row, (0, 128 - 3 * requests), constant_values=-16)
    columns = jnp.stack([from_row, info[0]], axis=1)
    tables = (
        table, weights, info, columns, taps, jnp.pad(dt_bias, pad)[None], jnp.pad(decay_rate, pad)[None],
        jnp.repeat(skip_gain, head_size)[None],
    )

    def inner(projected, parts, priors, tables):
        table, _, info, columns, taps, bias, decay, skip = tables
        sums = mixer_inner(
            z.reshape(1), table, parts, priors, projected, info, columns, taps,
            bias, decay, skip,
        )
        return sums, table

    states = jnp.swapaxes(ssm_pool.reshape(slots, heads * head_size, state_size), 1, 2)
    conv_bc = jnp.pad(conv_bc_pool.reshape(slots * 3, bc_cols), ((0, PRIOR - 12), (0, x_cols - bc_cols)))
    pool = jnp.concatenate(
        [states.reshape(slots * state_size, x_cols), conv_x_pool.reshape(slots * 3, x_cols), conv_bc]
    )
    late, (total, table) = gather(pool, tokens, tables, project, inner)
    return mixer_late(table, 4, late, total, NZ * tokens.shape[0])


def solution(mesh):
    in_specs = (
        P(("cache", "tp"), None), P(None, "tp"), P(None, None, "tp"), P(None, "tp"), P(None, "tp"),
        P(None, None, "tp"), P("tp"), P("tp"), P("tp"), P("cache", "tp", None, None), P("cache", None, "tp"),
        P("cache", None, None, "tp"), P(), P(), P("cache", None),
    )
    return jax.shard_map(
        shards, mesh=mesh, in_specs=in_specs, out_specs=P("cache", "tp"), check_vma=False
    )
```

```python
import jax
import jax.numpy as jnp
from jax import lax
from jax.experimental import pallas as pl
from jax.experimental.pallas import tpu as pltpu
from jax.sharding import PartitionSpec as P

NX, NY, NZ = 4, 4, 8
MOST = 60 * 1024 * 1024
TILE = 64
PRIOR = 16
PRIORS = NX * PRIOR
WIDE = 512
F32, BF16 = jnp.float32, jnp.bfloat16


def chip(y, x, c):
    return (y % NY) * 2 * NX + (x % NX) * 2 + c


def every():
    return [(y, x, c) for y in range(NY) for x in range(NX) for c in range(2)]


def first_round(step):
    return [(chip(y, x, c), chip(y + c * step, x + (1 - c) * step, c)) for y, x, c in every()]


def second_round(step):
    return [(chip(y, x, c), chip(y + (1 - c) * step, x + c * step, c)) for y, x, c in every()]


CORES = [(chip(y, x, c), chip(y, x, 1 - c)) for y, x, c in every()]


def over_z(value, step):
    return lax.ppermute(value, "tp", [(z, (z + step) % NZ) for z in range(NZ)])


def on_cache(value, pairs):
    return lax.ppermute(value, "cache", pairs)


def moved(name, sources, shapes, moves):
    def kernel(*refs):
        ins, (outs, held, sems) = refs[: len(sources)], (refs[len(sources) : -2], refs[-2], refs[-1])
        inward, outward, first = [], [], 0
        for k, (src, at, count, dst, to) in enumerate(moves):
            spot = held.at[pl.ds(first, count), :]
            inward.append(pltpu.make_async_copy(ins[src].at[pl.ds(at, count), :], spot, sems.at[2 * k]))
            outward.append(pltpu.make_async_copy(spot, outs[dst].at[pl.ds(to, count), :], sems.at[2 * k + 1]))
            first += count
        for copy in inward:
            copy.start()
        for before, after in zip(inward, outward):
            before.wait()
            after.start()
        for copy in outward:
            copy.wait()

    rows = sum(move[2] for move in moves)
    return pl.pallas_call(
        kernel,
        out_shape=[jax.ShapeDtypeStruct(shape, sources[0].dtype) for shape in shapes],
        in_specs=[pl.BlockSpec(memory_space=pltpu.HBM)] * len(sources),
        out_specs=[pl.BlockSpec(memory_space=pltpu.HBM)] * len(shapes),
        scratch_shapes=[
            pltpu.VMEM((rows, sources[0].shape[1]), sources[0].dtype),
            pltpu.SemaphoreType.DMA((2 * len(moves),)),
        ],
        compiler_params=pltpu.CompilerParams(vmem_limit_bytes=MOST),
        cost_estimate=pl.CostEstimate(flops=0, bytes_accessed=4000000, transcendentals=0),
        name=name,
    )(*sources)


def lined(nodes):
    states, cols = nodes[0].shape[0] - PRIOR, nodes[0].shape[1]
    moves = []
    for k in range(len(nodes)):
        moves.append((k, 0, states, 0, k * states))
        moves.append((k, states, PRIOR, 0, len(nodes) * states + k * PRIOR))
        moves.append((k, states, PRIOR, 1, k * PRIOR))
    shapes = [(len(nodes) * (states + PRIOR), cols), (len(nodes) * PRIOR, cols)]
    return moved("lined", nodes, shapes, moves)


def gathered_priors(lines):
    moves = [(k, line.shape[0] - PRIORS, PRIORS, 0, k * PRIORS) for k, line in enumerate(lines)]
    return moved("gathered_priors", lines, [(len(lines) * PRIORS, lines[0].shape[1])], moves)[0]


def halves(top, bottom, spare=0):
    rows, cols = (top.shape[0] - spare) // 2, top.shape[1]
    return moved("halves", [top, bottom], [(rows, cols)] * 2, [(0, 0, rows, 0, 0), (1, rows, rows, 1, 0)])


def gather(pool, tokens, tables, project, inner):
    tie = lax.optimization_barrier
    near_up, near_down = on_cache(pool, first_round(1)), on_cache(pool, first_round(-1))
    far = on_cache(pool, first_round(2))
    up, down = over_z(tokens, 1), over_z(tokens, -1)
    blocks = [tokens, up, down]
    up, down = over_z(up, 1), over_z(down, -1)
    blocks += [up, down]
    near_up, near_down, far, tables = tie((near_up, near_down, far, tables))
    line, line_prior = lined([pool, near_up, near_down, far])
    line, line_prior, up, down, blocks = tie((line, line_prior, up, down, blocks))

    near_up, near_down = on_cache(line, second_round(1)), on_cache(line, second_round(-1))
    far_prior = on_cache(line_prior, second_round(2))
    to_send, far_prior = tie((line, far_prior))
    line_other = on_cache(to_send, CORES)
    projected = [project(blocks, tables[1], 24000000000)]
    up, down = over_z(up, 1), over_z(down, -1)
    up, down, projected = tie((up, down, projected))
    last_up, last_down = halves(up, down)
    blocks = [up, down, over_z(last_up, 1), over_z(last_down, -1)]
    near_up, near_down, far_prior, up, down = tie((near_up, near_down, far_prior, up, down))

    priors = gathered_priors([line_prior, near_up, near_down, far_prior])
    far_up, far_down = halves(near_up, near_down, PRIORS)
    far_up, far_down = on_cache(far_up, second_round(1)), on_cache(far_down, second_round(-1))
    priors = [priors, on_cache(priors, CORES)]
    blocks, line_other = tie((blocks, line_other))
    projected.append(project(blocks, tables[1], 24000000000))
    near_up, near_down, projected = tie((near_up, near_down, projected))
    up_other, down_other = on_cache(near_up, CORES), on_cache(near_down, CORES)
    result = inner(projected, [line, line_other, near_up, near_down], priors, tables)
    far_up, far_down, result = tie((far_up, far_down, result))
    far_others = [on_cache(far_up, CORES), on_cache(far_down, CORES)]
    return [up_other, down_other, far_up, far_others[0], far_down, far_others[1]], result


def dot(a, b):
    return jnp.dot(a, b, preferred_element_type=F32)


def dot_t(a, b):
    return lax.dot_general(a, b, (((1,), (1,)), ((), ())), preferred_element_type=F32)


def fetched(blocks, weights, tok, held, sem):
    w_x_in, w_bc_in, w_dt_in = weights
    w_x, w_bc, w_dt = held
    now, at = [], 0
    for block in blocks:
        now.append(pltpu.make_async_copy(block, tok.at[pl.ds(at, block.shape[0]), :], sem.at[len(now)]))
        at += block.shape[0]
    heads = w_dt_in.shape[0]
    now.append(pltpu.make_async_copy(w_bc_in, w_bc, sem.at[len(now)]))
    now.append(pltpu.make_async_copy(w_dt_in, w_dt.at[pl.ds(0, heads), :], sem.at[len(now)]))
    chunks = []
    for k in range(w_x.shape[1] // WIDE):
        here = (slice(None), slice(WIDE * k, WIDE * (k + 1)))
        chunks.append(pltpu.make_async_copy(w_x_in.at[here], w_x.at[here], sem.at[len(now) + k]))
    for copy in now + chunks:
        copy.start()
    w_dt[heads:, :] = jnp.zeros((128 - heads, w_dt.shape[1]), BF16)
    return now, chunks


def project_kernel(*refs):
    blocks, (w_x_in, w_bc_in, w_dt_in, x_out, b_out, tok, w_x, w_bc, w_dt, sem) = refs[:-10], refs[-10:]
    now, chunks = fetched(blocks, (w_x_in, w_bc_in, w_dt_in), tok, (w_x, w_bc, w_dt), sem)
    for copy in now:
        copy.wait()
    b_out[:, 0:256] = dot(tok[...], w_bc[...]).astype(BF16)
    b_out[:, 256:384] = dot_t(tok[...], w_dt[...]).astype(BF16)
    for k, copy in enumerate(chunks):
        copy.wait()
        here = slice(WIDE * k, WIDE * (k + 1))
        x_out[:, here] = dot(tok[...], w_x[:, here]).astype(BF16)


def inner_kernel(
    where, table, s0, s1, s2, s3, p0, p1, x_first, b_first, x_next, b_next, info, cols_in, taps, bias, decay, skip, sum_ref,
    raw, xs, bs, cs, run, step, states, state_sem, prior, prior_sem,
):
    rows = raw.shape[0] - 8
    columns = cols_in[...].T
    x_cols = xs.shape[1]
    c_ref, fade_ref = sum_ref.at[x_cols // 128], sum_ref.at[x_cols // 128 + 1]
    cols = taps.shape[1]
    block = rows // NZ
    z = where[0]
    now = []
    parts = (s0, s1, s2, s3)
    fetch_states(table, 0, parts, states, state_sem)
    for k, source in enumerate((p0, p1)):
        spot = prior.at[pl.ds(k * p0.shape[0], p0.shape[0]), :]
        now.append(pltpu.make_async_copy(source, spot, prior_sem.at[k]))
        now[-1].start()

    def put(target, lead, columns, values, shifts):
        for k, shift in enumerate(shifts):
            at = pl.multiple_of(lax.rem(z + shift + NZ, NZ) * block, block)
            target[pl.ds(lead + at, block), columns] = values[k * block : (k + 1) * block].astype(F32)

    put(raw, 8, slice(0, x_cols), x_first, (0, -1, 1, -2, 2))
    put(raw, 8, slice(x_cols, cols), b_first[:, 0:256], (0, -1, 1, -2, 2))
    put(step, TILE, slice(None), b_first[:, 256:384], (0, -1, 1, -2, 2))
    put(raw, 8, slice(0, x_cols), x_next, (-3, 3, 4))
    put(raw, 8, slice(x_cols, cols), b_next[:, 0:256], (-3, 3, 4))
    put(step, TILE, slice(None), b_next[:, 256:384], (-3, 3, 4))
    raw[0:8, :] = jnp.zeros((8, cols), F32)

    position = lax.broadcasted_iota(jnp.int32, (rows, 128), 0)
    request = lax.broadcasted_iota(jnp.int32, (rows, 128), 1).astype(F32)
    req_col = jnp.sum(jnp.where(position >= info[0:1, :], 1.0, 0.0), axis=1, keepdims=True)
    is_own = request == req_col
    own_start = jnp.sum(jnp.where(is_own, info[1:2, :].astype(F32), 0.0), axis=1, keepdims=True)
    offset = position[:, 0:1].astype(F32) - own_start

    def requests_at(first, count):
        spot = first + lax.broadcasted_iota(jnp.int32, (info.shape[1], count), 1)
        found = jnp.sum(jnp.where(spot.astype(F32) >= columns[:, 1:2], 1.0, 0.0), axis=0, keepdims=True)
        return jnp.where(spot[0:1] < 0, -1.0, found)

    before = lax.broadcasted_iota(jnp.int32, (rows, rows), 0) >= lax.broadcasted_iota(
        jnp.int32, (rows, rows), 1
    )
    sums = jnp.where((req_col == requests_at(0, rows)) & before, 1.0, 0.0).astype(BF16)
    slot_ids = lax.broadcasted_iota(jnp.int32, (columns.shape[0], prior.shape[0]), 1).astype(F32)
    pick_x = jnp.where(slot_ids == columns[:, 0:1], 1.0, 0.0).astype(BF16)
    pick_bc = jnp.where(slot_ids == columns[:, 0:1] + 6, 1.0, 0.0).astype(BF16)
    spot_ids = lax.broadcasted_iota(jnp.int32, (rows, columns.shape[0]), 1).astype(F32)
    chosen = [
        jnp.where((spot_ids == 3 * req_col + offset + (3 - lag)) & (offset < lag), 1.0, 0.0).astype(BF16)
        for lag in (1, 2, 3)
    ]
    xs[0:TILE, :] = jnp.zeros((TILE, x_cols), BF16)
    bs[0:TILE, :] = jnp.zeros((TILE, 128), BF16)
    run[0:TILE, :] = jnp.zeros((TILE, 128), F32)
    step[0:TILE, :] = jnp.zeros((TILE, 128), F32)
    c_ref[rows:, :] = jnp.zeros((c_ref.shape[0] - rows, 128), F32)

    def convolved(here, inputs):
        total = taps[3:4, here] * raw[8:, here]
        for lag in (1, 2, 3):
            shifted = raw[8 - lag : 8 - lag + rows, here]
            value = jnp.where(offset < lag, 0.0, shifted) + dot(chosen[lag - 1], inputs)
            total = total + taps[3 - lag : 4 - lag, here] * value
        return (total / (1.0 + jnp.exp(-total))).astype(BF16)

    for copy in now:
        copy.wait()
    out = convolved(slice(x_cols, cols), dot(pick_bc, prior[:, 0 : cols - x_cols]).astype(BF16))
    inputs = dot(pick_x, prior[...]).astype(BF16)
    bs[TILE:, :] = out[:, 0:128]
    cs[...] = out[:, 128:256]
    c_ref[0:rows, :] = out[:, 128:256].astype(F32)
    steps = jax.nn.softplus(step[TILE:, :] + bias[...])
    step[TILE:, :] = steps
    log_keep = -steps * decay[...]
    high = log_keep.astype(BF16)
    left = log_keep - high.astype(F32)
    middle = left.astype(BF16)
    low = (left - middle.astype(F32)).astype(BF16)
    running = dot(sums, high) + dot(sums, middle) + dot(sums, low)
    run[TILE:, :] = running
    fade_ref[0:rows, :] = jnp.exp(running)

    for at in range(0, x_cols, 256):
        xs[TILE:, at : at + 256] = convolved(slice(at, at + 256), inputs[:, at : at + 256])

    lanes = lax.broadcasted_iota(jnp.int32, (TILE, 2 * TILE), 1)
    subs = lax.broadcasted_iota(jnp.int32, (TILE, 2 * TILE), 0)
    left = lax.broadcasted_iota(jnp.int32, (2 * TILE, 128), 1) < 64

    def tile(j, carry):
        at = pl.multiple_of(j * TILE, TILE)
        score = dot_t(cs[pl.ds(at, TILE), :], bs[pl.ds(at, 2 * TILE), :])
        around = requests_at(at - TILE, 2 * TILE)
        own = around.reshape(1, 2 * TILE)
        own_col = jnp.sum(
            jnp.where(at + subs >= info[0:1, :], 1.0, 0.0), axis=1, keepdims=True
        )
        mask = (own_col == own) & (lanes - TILE <= subs)
        run_w = run[pl.ds(at, 2 * TILE), :]
        run_rows = run_w.T
        step_rows = step[pl.ds(at, 2 * TILE), :].T
        run_cols = run_w[TILE:, :]
        for pair in range(x_cols // 128):
            mixes = []
            for h in (2 * pair, 2 * pair + 1):
                gap = run_cols[:, h : h + 1] - run_rows[h : h + 1, :]
                mix = jnp.exp(jnp.where(mask, gap, -jnp.inf)) * score * step_rows[h : h + 1, :]
                mixes.append(mix.astype(BF16))
            here = slice(128 * pair, 128 * (pair + 1))
            x_w = xs[pl.ds(at, 2 * TILE), here]
            nothing = jnp.zeros_like(x_w)
            both = jnp.concatenate([jnp.where(left, x_w, nothing), jnp.where(left, nothing, x_w)], axis=0)
            out = dot(jnp.concatenate(mixes, axis=1), both)
            sum_ref[pair, pl.ds(at, TILE), :] = out + skip[:, here] * x_w[TILE:].astype(F32)
        return carry

    lax.fori_loop(0, rows // TILE, tile, 0)
    sum_ref[0 : x_cols // 128, rows:, :] = jnp.zeros((x_cols // 128, sum_ref.shape[1] - rows, 128), F32)
    fade_ref[rows:, :] = jnp.zeros((fade_ref.shape[0] - rows, 128), F32)
    add_carried(table, 0, parts, c_ref, fade_ref, states, sum_ref, state_sem)


def fetch_states(table, first, arrays, states, sems):
    state_size = states.shape[1]
    for k, array in enumerate(arrays):

        def begin(i, carry, array=array):
            at = pl.multiple_of(table[2, i] * state_size, state_size)
            pltpu.make_async_copy(array.at[pl.ds(at, state_size), :], states.at[i], sems.at[i]).start()
            return carry

        lax.fori_loop(table[3, first + k], table[3, first + k + 1], begin, 0)


def add_carried(table, first, arrays, c_ref, fade_ref, states, total, sems):
    requests, state_size, x_cols = states.shape
    begins, ends = table[3, first], table[3, first + len(arrays)]
    row = lax.broadcasted_iota(jnp.int32, (32, 128), 0)
    lane_head = lax.broadcasted_iota(jnp.int32, (128, x_cols), 1) // 64
    spread = jnp.where(lane_head == lax.broadcasted_iota(jnp.int32, (128, x_cols), 0), 1.0, 0.0).astype(BF16)
    side = 4

    def some(group, carry):
        picks = []
        for k in range(side):
            i = begins + group * side + k

            @pl.when(i < ends)
            def _():
                pltpu.make_async_copy(
                    arrays[0].at[pl.ds(0, state_size), :], states.at[i], sems.at[i]
                ).wait()

            safe = jnp.minimum(i, requests - 1)
            picks.append((safe, table[0, safe], jnp.where(i < ends, table[1, safe], 0)))
        terms = []
        for i, start, _ in picks:
            fade = fade_ref[pl.ds(start, 32), :]
            high = fade.astype(BF16)
            low = (fade - high.astype(F32)).astype(BF16)
            scale = dot(jnp.concatenate([high, low], axis=0), spread)
            product = dot(c_ref[pl.ds(start, 32), :].astype(BF16), states[i])
            terms.append((scale[0:32] + scale[32:64]) * product)
        for term, (_, start, length) in zip(terms, picks):
            inside = row < length
            for k in range(x_cols // 128):
                old = total[k, pl.ds(start, 32), :]
                total[k, pl.ds(start, 32), :] = jnp.where(
                    inside, old + term[:, 128 * k : 128 * (k + 1)], old
                )
        return carry

    lax.fori_loop(0, lax.div(ends - begins + side - 1, side), some, 0)


def late_kernel(first, count, table, *refs):
    arrays, (before, out, states, total, sems, got) = refs[:count], refs[count:]
    rows, x_cols = out.shape
    c_ref, fade_ref = total.at[x_cols // 128], total.at[x_cols // 128 + 1]
    copy = pltpu.make_async_copy(before, total, got)
    copy.start()
    fetch_states(table, first, arrays, states, sems)
    copy.wait()
    add_carried(table, first, arrays, c_ref, fade_ref, states, total, sems)
    for k in range(x_cols // 128):
        out[:, 128 * k : 128 * (k + 1)] = total[k, 0:rows, :].astype(BF16)


VMEM = pl.BlockSpec(memory_space=pltpu.VMEM)
SMEM = pl.BlockSpec(memory_space=pltpu.SMEM)
HBM = pl.BlockSpec(memory_space=pltpu.HBM)
ANY = pl.BlockSpec(memory_space=pl.ANY)


def weight_scratch(weights, rows, copies):
    depth, x_cols = weights[0].shape
    return [
        pltpu.VMEM((rows, depth), BF16),
        pltpu.VMEM((depth, x_cols), BF16),
        pltpu.VMEM((depth, weights[1].shape[1]), BF16),
        pltpu.VMEM((128, depth), BF16),
        pltpu.SemaphoreType.DMA((copies + 2 + x_cols // WIDE,)),
    ]


def project(blocks, weights, flops):
    rows, x_cols = sum(b.shape[0] for b in blocks), weights[0].shape[1]
    return pl.pallas_call(
        project_kernel,
        out_shape=(
            jax.ShapeDtypeStruct((rows, x_cols), BF16),
            jax.ShapeDtypeStruct((rows, weights[1].shape[1] + 128), BF16),
        ),
        in_specs=[HBM] * (len(blocks) + 3),
        out_specs=(VMEM, VMEM),
        scratch_shapes=weight_scratch(weights, rows, len(blocks)),
        compiler_params=pltpu.CompilerParams(vmem_limit_bytes=MOST),
        cost_estimate=pl.CostEstimate(flops=flops, bytes_accessed=14000000, transcendentals=0),
        name="project",
    )(*blocks, *weights)


def mixer_inner(z, table, parts, priors, projected, info, columns, taps, bias, decay, skip):
    rows = sum(p[0].shape[0] for p in projected)
    x_cols, cols = projected[0][0].shape[1], taps.shape[1]
    requests, state_size, margin = table.shape[1] - 1, 128, 32
    return pl.pallas_call(
        inner_kernel,
        out_shape=jax.ShapeDtypeStruct((x_cols // 128 + 2, rows + margin, 128), F32),
        in_specs=[SMEM] * 2 + [HBM] * 6 + [VMEM] * 10,
        out_specs=VMEM,
        scratch_shapes=[
            pltpu.VMEM((rows + 8, cols), F32),
            pltpu.VMEM((rows + TILE, x_cols), BF16),
            pltpu.VMEM((rows + TILE, 128), BF16),
            pltpu.VMEM((rows, 128), BF16),
            pltpu.VMEM((rows + TILE, 128), F32),
            pltpu.VMEM((rows + TILE, 128), F32),
            pltpu.VMEM((requests, state_size, x_cols), BF16),
            pltpu.SemaphoreType.DMA((requests,)),
            pltpu.VMEM((8 * PRIORS, x_cols), BF16),
            pltpu.SemaphoreType.DMA((2,)),
        ],
        compiler_params=pltpu.CompilerParams(vmem_limit_bytes=MOST),
        cost_estimate=pl.CostEstimate(flops=14000000000, bytes_accessed=18000000, transcendentals=2000000),
        name="mixer_inner",
    )(z, table, *parts, *priors, *projected[0], *projected[1], info, columns, taps, bias, decay, skip)


def mixer_late(table, first, arrays, total, rows):
    x_cols = (total.shape[0] - 2) * 128
    state_size, requests = total.shape[2], table.shape[1] - 1
    return pl.pallas_call(
        lambda *refs: late_kernel(first, len(arrays), *refs),
        out_shape=jax.ShapeDtypeStruct((rows, x_cols), BF16),
        in_specs=[SMEM] + [ANY] * (len(arrays) + 1),
        out_specs=VMEM,
        scratch_shapes=[
            pltpu.VMEM((requests, state_size, x_cols), BF16),
            pltpu.VMEM(total.shape, F32),
            pltpu.SemaphoreType.DMA((requests,)),
            pltpu.SemaphoreType.DMA,
        ],
        compiler_params=pltpu.CompilerParams(vmem_limit_bytes=24 * 1024 * 1024),
        cost_estimate=pl.CostEstimate(flops=500000000, bytes_accessed=13000000, transcendentals=0),
        name="mixer_late",
    )(table, *arrays, total)


def shards(
    tokens, weight_x, weight_bc, weight_dt, kernel_x, kernel_bc, dt_bias, decay_rate, skip_gain,
    ssm_pool, conv_x_pool, conv_bc_pool, hit_holder, hit_slot, suffix_len,
):
    model_dim, heads = weight_dt.shape
    x_cols = weight_x.shape[1]
    bc_cols = weight_bc.shape[1] * weight_bc.shape[2]
    slots, head_size, state_size = ssm_pool.shape[0], ssm_pool.shape[2], ssm_pool.shape[3]
    requests = suffix_len.shape[1]
    me, z = lax.axis_index("cache"), lax.axis_index("tp")

    weights = (weight_x, weight_bc.reshape(model_dim, bc_cols), weight_dt.T)

    lengths = suffix_len[0]
    order = jnp.arange(requests, dtype=jnp.int32)
    ends = jnp.sum(jnp.where(order[None, :] <= order[:, None], lengths[None, :], 0), axis=1)
    starts = ends - lengths
    holder = lax.dynamic_slice_in_dim(hit_holder[:, 0], me * requests, requests)
    slot = lax.dynamic_slice_in_dim(hit_slot, me * requests, requests)
    my_y, my_x, my_c = me // (2 * NX), (me // 2) % NX, me % 2
    at_y, at_x, at_c = holder // (2 * NX), (holder // 2) % NX, holder % 2
    far_y, far_x = (my_y - at_y) % NY, (my_x - at_x) % NX
    outer, inner = jnp.where(at_c == 0, far_y, far_x), jnp.where(at_c == 0, far_x, far_y)
    node = jnp.where(inner == 2, 3, jnp.where(inner == 3, 2, inner))
    line = jnp.where(outer == 2, 3, jnp.where(outer == 3, 2, outer))
    prior_row = ((at_c != my_c) * NY + line) * PRIORS + node * PRIOR + slot * 3
    block = 2 * node + slot
    part_of = jnp.where(outer == 2, 3 + block // 4, line)
    block = jnp.where(outer == 2, block % 4, block)
    own = at_c == my_c
    array = jnp.where(
        part_of < 3,
        jnp.where(part_of == 0, jnp.where(own, 0, 1), jnp.where(own, 1, 3) + part_of),
        jnp.where(own, 0, 1) + 2 * part_of,
    )
    key = array * requests + order
    rank = jnp.sum((key[None, :] < key[:, None]).astype(jnp.int32), axis=1)
    sorting = (rank[None, :] == order[:, None]).astype(jnp.int32)
    by_array = jnp.sum(sorting[None] * jnp.stack([starts, lengths, block])[:, None, :], axis=2)
    firsts = jnp.sum((array[None, :] < order[:, None]).astype(jnp.int32), axis=1)
    table = jnp.concatenate([by_array, firsts[None]], axis=0).astype(jnp.int32)
    table = jnp.pad(table, ((0, 0), (0, 1)))
    info = jnp.stack([ends, starts])
    info = jnp.concatenate([info, jnp.full((2, 128 - requests), 1 << 20, jnp.int32)], axis=1)

    taps = jnp.concatenate([kernel_x, kernel_bc.reshape(4, bc_cols)], axis=1).astype(F32)
    pad = (0, 128 - heads)
    from_row = (prior_row[:, None] + jnp.arange(3)[None, :]).reshape(-1)
    from_row = jnp.pad(from_row, (0, 128 - 3 * requests), constant_values=-16)
    columns = jnp.pad(jnp.stack([from_row, info[0]]).astype(F32), ((0, 6), (0, 0)))
    tables = (
        table, weights, info, columns, taps, jnp.pad(dt_bias, pad)[None], jnp.pad(decay_rate, pad)[None],
        jnp.repeat(skip_gain, head_size)[None],
    )

    def inner(projected, parts, priors, tables):
        table, _, info, columns, taps, bias, decay, skip = tables
        sums = mixer_inner(
            z.reshape(1), table, parts, priors, projected, info, columns, taps,
            bias, decay, skip,
        )
        return sums, table

    states = jnp.swapaxes(ssm_pool.reshape(slots, heads * head_size, state_size), 1, 2)
    conv_bc = jnp.pad(conv_bc_pool.reshape(slots * 3, bc_cols), ((0, PRIOR - 12), (0, x_cols - bc_cols)))
    pool = jnp.concatenate(
        [states.reshape(slots * state_size, x_cols), conv_x_pool.reshape(slots * 3, x_cols), conv_bc]
    )
    late, (total, table) = gather(pool, tokens, tables, project, inner)
    return mixer_late(table, 4, late, total, NZ * tokens.shape[0])


def solution(mesh):
    in_specs = (
        P(("cache", "tp"), None), P(None, "tp"), P(None, None, "tp"), P(None, "tp"), P(None, "tp"),
        P(None, None, "tp"), P("tp"), P("tp"), P("tp"), P("cache", "tp", None, None), P("cache", None, "tp"),
        P("cache", None, None, "tp"), P(), P(), P("cache", None),
    )
    return jax.shard_map(
        shards, mesh=mesh, in_specs=in_specs, out_specs=P("cache", "tp"), check_vma=False
    )
```

```python
import jax
import jax.numpy as jnp
from jax import lax
from jax.experimental import pallas as pl
from jax.experimental.pallas import tpu as pltpu
from jax.sharding import PartitionSpec as P

NX, NY, NZ = 4, 4, 8
MOST = 60 * 1024 * 1024
TILE = 64
PRIOR = 16
PRIORS = NX * PRIOR
WIDE = 512
F32, BF16 = jnp.float32, jnp.bfloat16


def chip(y, x, c):
    return (y % NY) * 2 * NX + (x % NX) * 2 + c


def every():
    return [(y, x, c) for y in range(NY) for x in range(NX) for c in range(2)]


def first_round(step):
    return [(chip(y, x, c), chip(y + c * step, x + (1 - c) * step, c)) for y, x, c in every()]


def second_round(step):
    return [(chip(y, x, c), chip(y + (1 - c) * step, x + c * step, c)) for y, x, c in every()]


CORES = [(chip(y, x, c), chip(y, x, 1 - c)) for y, x, c in every()]


def over_z(value, step):
    return lax.ppermute(value, "tp", [(z, (z + step) % NZ) for z in range(NZ)])


def on_cache(value, pairs):
    return lax.ppermute(value, "cache", pairs)


def moved(name, sources, shapes, moves):
    def kernel(*refs):
        ins, (outs, held, sems) = refs[: len(sources)], (refs[len(sources) : -2], refs[-2], refs[-1])
        inward, outward, first = [], [], 0
        for k, (src, at, count, dst, to) in enumerate(moves):
            spot = held.at[pl.ds(first, count), :]
            inward.append(pltpu.make_async_copy(ins[src].at[pl.ds(at, count), :], spot, sems.at[2 * k]))
            outward.append(pltpu.make_async_copy(spot, outs[dst].at[pl.ds(to, count), :], sems.at[2 * k + 1]))
            first += count
        for copy in inward:
            copy.start()
        for before, after in zip(inward, outward):
            before.wait()
            after.start()
        for copy in outward:
            copy.wait()

    rows = sum(move[2] for move in moves)
    return pl.pallas_call(
        kernel,
        out_shape=[jax.ShapeDtypeStruct(shape, sources[0].dtype) for shape in shapes],
        in_specs=[pl.BlockSpec(memory_space=pltpu.HBM)] * len(sources),
        out_specs=[pl.BlockSpec(memory_space=pltpu.HBM)] * len(shapes),
        scratch_shapes=[
            pltpu.VMEM((rows, sources[0].shape[1]), sources[0].dtype),
            pltpu.SemaphoreType.DMA((2 * len(moves),)),
        ],
        compiler_params=pltpu.CompilerParams(vmem_limit_bytes=MOST),
        cost_estimate=pl.CostEstimate(flops=0, bytes_accessed=4000000, transcendentals=0),
        name=name,
    )(*sources)


def lined(nodes):
    states, cols = nodes[0].shape[0] - PRIOR, nodes[0].shape[1]
    moves = []
    for k in range(len(nodes)):
        moves.append((k, 0, states, 0, k * states))
        moves.append((k, states, PRIOR, 0, len(nodes) * states + k * PRIOR))
        moves.append((k, states, PRIOR, 1, k * PRIOR))
    shapes = [(len(nodes) * (states + PRIOR), cols), (len(nodes) * PRIOR, cols)]
    return moved("lined", nodes, shapes, moves)


def gathered_priors(lines):
    moves = [(k, line.shape[0] - PRIORS, PRIORS, 0, k * PRIORS) for k, line in enumerate(lines)]
    return moved("gathered_priors", lines, [(len(lines) * PRIORS, lines[0].shape[1])], moves)[0]


def halves(top, bottom, spare=0):
    rows, cols = (top.shape[0] - spare) // 2, top.shape[1]
    return moved("halves", [top, bottom], [(rows, cols)] * 2, [(0, 0, rows, 0, 0), (1, rows, rows, 1, 0)])


def gather(pool, tokens, tables, project, inner):
    tie = lax.optimization_barrier
    near_up, near_down = on_cache(pool, first_round(1)), on_cache(pool, first_round(-1))
    far = on_cache(pool, first_round(2))
    up, down = over_z(tokens, 1), over_z(tokens, -1)
    blocks = [tokens, up, down]
    up, down = over_z(up, 1), over_z(down, -1)
    blocks += [up, down]
    near_up, near_down, far, tables = tie((near_up, near_down, far, tables))
    line, line_prior = lined([pool, near_up, near_down, far])
    line, line_prior, up, down, blocks = tie((line, line_prior, up, down, blocks))

    near_up, near_down = on_cache(line, second_round(1)), on_cache(line, second_round(-1))
    far_prior = on_cache(line_prior, second_round(2))
    to_send, far_prior = tie((line, far_prior))
    line_other = on_cache(to_send, CORES)
    projected = [project(blocks, tables[1], 24000000000)]
    up, down = over_z(up, 1), over_z(down, -1)
    up, down, projected = tie((up, down, projected))
    last_up, last_down = halves(up, down)
    blocks = [up, down, over_z(last_up, 1), over_z(last_down, -1)]
    near_up, near_down, far_prior, up, down = tie((near_up, near_down, far_prior, up, down))

    priors = gathered_priors([line_prior, near_up, near_down, far_prior])
    far_up, far_down = halves(near_up, near_down, PRIORS)
    far_up, far_down = on_cache(far_up, second_round(1)), on_cache(far_down, second_round(-1))
    priors = [priors, on_cache(priors, CORES)]
    blocks, line_other = tie((blocks, line_other))
    projected.append(project(blocks, tables[1], 24000000000))
    near_up, near_down, projected = tie((near_up, near_down, projected))
    up_other, down_other = on_cache(near_up, CORES), on_cache(near_down, CORES)
    result = inner(projected, [line, line_other, near_up, near_down], priors, tables)
    far_up, far_down, result = tie((far_up, far_down, result))
    far_others = [on_cache(far_up, CORES), on_cache(far_down, CORES)]
    return [up_other, down_other, far_up, far_others[0], far_down, far_others[1]], result


def dot(a, b):
    return jnp.dot(a, b, preferred_element_type=F32)


def dot_t(a, b):
    return lax.dot_general(a, b, (((1,), (1,)), ((), ())), preferred_element_type=F32)


def fetched(blocks, weights, tok, held, sem):
    w_x_in, w_bc_in, w_dt_in = weights
    w_x, w_bc, w_dt = held
    now, at = [], 0
    for block in blocks:
        now.append(pltpu.make_async_copy(block, tok.at[pl.ds(at, block.shape[0]), :], sem.at[len(now)]))
        at += block.shape[0]
    heads = w_dt_in.shape[0]
    now.append(pltpu.make_async_copy(w_bc_in, w_bc, sem.at[len(now)]))
    now.append(pltpu.make_async_copy(w_dt_in, w_dt.at[pl.ds(0, heads), :], sem.at[len(now)]))
    chunks = []
    for k in range(w_x.shape[1] // WIDE):
        here = (slice(None), slice(WIDE * k, WIDE * (k + 1)))
        chunks.append(pltpu.make_async_copy(w_x_in.at[here], w_x.at[here], sem.at[len(now) + k]))
    for copy in now + chunks:
        copy.start()
    w_dt[heads:, :] = jnp.zeros((128 - heads, w_dt.shape[1]), BF16)
    return now, chunks


def project_kernel(*refs):
    blocks, (w_x_in, w_bc_in, w_dt_in, x_out, b_out, tok, w_x, w_bc, w_dt, sem) = refs[:-10], refs[-10:]
    now, chunks = fetched(blocks, (w_x_in, w_bc_in, w_dt_in), tok, (w_x, w_bc, w_dt), sem)
    for copy in now:
        copy.wait()
    b_out[:, 0:256] = dot(tok[...], w_bc[...]).astype(BF16)
    b_out[:, 256:384] = dot_t(tok[...], w_dt[...]).astype(BF16)
    for k, copy in enumerate(chunks):
        copy.wait()
        here = slice(WIDE * k, WIDE * (k + 1))
        x_out[:, here] = dot(tok[...], w_x[:, here]).astype(BF16)


def inner_kernel(
    where, table, s0, s1, s2, s3, p0, p1, x_first, b_first, x_next, b_next, info, cols_in, taps, bias, decay, skip, sum_ref,
    raw, xs, bs, cs, run, step, states, state_sem, prior, prior_sem,
):
    rows = raw.shape[0] - 8
    columns = cols_in[...].T
    x_cols = xs.shape[1]
    c_ref, fade_ref = sum_ref.at[x_cols // 128], sum_ref.at[x_cols // 128 + 1]
    cols = taps.shape[1]
    block = rows // NZ
    z = where[0]
    now = []
    parts = (s0, s1, s2, s3)
    fetch_states(table, 0, parts, states, state_sem)
    for k, source in enumerate((p0, p1)):
        spot = prior.at[pl.ds(k * p0.shape[0], p0.shape[0]), :]
        now.append(pltpu.make_async_copy(source, spot, prior_sem.at[k]))
        now[-1].start()

    def put(target, lead, columns, values, shifts):
        for k, shift in enumerate(shifts):
            at = pl.multiple_of(lax.rem(z + shift + NZ, NZ) * block, block)
            target[pl.ds(lead + at, block), columns] = values[k * block : (k + 1) * block].astype(F32)

    put(raw, 8, slice(0, x_cols), x_first, (0, -1, 1, -2, 2))
    put(raw, 8, slice(x_cols, cols), b_first[:, 0:256], (0, -1, 1, -2, 2))
    put(step, TILE, slice(None), b_first[:, 256:384], (0, -1, 1, -2, 2))
    put(raw, 8, slice(0, x_cols), x_next, (-3, 3, 4))
    put(raw, 8, slice(x_cols, cols), b_next[:, 0:256], (-3, 3, 4))
    put(step, TILE, slice(None), b_next[:, 256:384], (-3, 3, 4))
    raw[0:8, :] = jnp.zeros((8, cols), F32)

    position = lax.broadcasted_iota(jnp.int32, (rows, 128), 0)
    request = lax.broadcasted_iota(jnp.int32, (rows, 128), 1).astype(F32)
    req_col = jnp.sum(jnp.where(position >= info[0:1, :], 1.0, 0.0), axis=1, keepdims=True)
    is_own = request == req_col
    own_start = jnp.sum(jnp.where(is_own, info[1:2, :].astype(F32), 0.0), axis=1, keepdims=True)
    offset = position[:, 0:1].astype(F32) - own_start

    def requests_at(first, count):
        spot = first + lax.broadcasted_iota(jnp.int32, (info.shape[1], count), 1)
        found = jnp.sum(jnp.where(spot.astype(F32) >= columns[:, 1:2], 1.0, 0.0), axis=0, keepdims=True)
        return jnp.where(spot[0:1] < 0, -1.0, found)

    before = lax.broadcasted_iota(jnp.int32, (rows, rows), 0) >= lax.broadcasted_iota(
        jnp.int32, (rows, rows), 1
    )
    sums = jnp.where((req_col == requests_at(0, rows)) & before, 1.0, 0.0).astype(BF16)
    slot_ids = lax.broadcasted_iota(jnp.int32, (columns.shape[0], prior.shape[0]), 1).astype(F32)
    pick_x = jnp.where(slot_ids == columns[:, 0:1], 1.0, 0.0).astype(BF16)
    pick_bc = jnp.where(slot_ids == columns[:, 0:1] + 6, 1.0, 0.0).astype(BF16)
    spot_ids = lax.broadcasted_iota(jnp.int32, (rows, columns.shape[0]), 1).astype(F32)
    chosen = [
        jnp.where((spot_ids == 3 * req_col + offset + (3 - lag)) & (offset < lag), 1.0, 0.0).astype(BF16)
        for lag in (1, 2, 3)
    ]
    xs[0:TILE, :] = jnp.zeros((TILE, x_cols), BF16)
    bs[0:TILE, :] = jnp.zeros((TILE, 128), BF16)
    run[0:TILE, :] = jnp.zeros((TILE, 128), F32)
    step[0:TILE, :] = jnp.zeros((TILE, 128), F32)
    c_ref[rows:, :] = jnp.zeros((c_ref.shape[0] - rows, 128), F32)

    def convolved(here, inputs):
        total = taps[3:4, here] * raw[8:, here]
        for lag in (1, 2, 3):
            shifted = raw[8 - lag : 8 - lag + rows, here]
            value = jnp.where(offset < lag, 0.0, shifted) + dot(chosen[lag - 1], inputs)
            total = total + taps[3 - lag : 4 - lag, here] * value
        return (total / (1.0 + jnp.exp(-total))).astype(BF16)

    for copy in now:
        copy.wait()
    out = convolved(slice(x_cols, cols), dot(pick_bc, prior[:, 0 : cols - x_cols]).astype(BF16))
    inputs = dot(pick_x, prior[...]).astype(BF16)
    bs[TILE:, :] = out[:, 0:128]
    cs[...] = out[:, 128:256]
    c_ref[0:rows, :] = out[:, 128:256].astype(F32)
    steps = jax.nn.softplus(step[TILE:, :] + bias[...])
    step[TILE:, :] = steps
    log_keep = -steps * decay[...]
    high = log_keep.astype(BF16)
    left = log_keep - high.astype(F32)
    middle = left.astype(BF16)
    low = (left - middle.astype(F32)).astype(BF16)
    running = dot(sums, high) + dot(sums, middle) + dot(sums, low)
    run[TILE:, :] = running
    fade_ref[0:rows, :] = jnp.exp(running)

    for at in range(0, x_cols, 256):
        xs[TILE:, at : at + 256] = convolved(slice(at, at + 256), inputs[:, at : at + 256])

    lanes = lax.broadcasted_iota(jnp.int32, (TILE, 2 * TILE), 1)
    subs = lax.broadcasted_iota(jnp.int32, (TILE, 2 * TILE), 0)
    left = lax.broadcasted_iota(jnp.int32, (2 * TILE, 128), 1) < 64

    def tile(j, carry):
        at = pl.multiple_of(j * TILE, TILE)
        score = dot_t(cs[pl.ds(at, TILE), :], bs[pl.ds(at, 2 * TILE), :])
        around = requests_at(at - TILE, 2 * TILE)
        own = around.reshape(1, 2 * TILE)
        own_col = jnp.sum(
            jnp.where(at + subs >= info[0:1, :], 1.0, 0.0), axis=1, keepdims=True
        )
        mask = (own_col == own) & (lanes - TILE <= subs)
        run_w = run[pl.ds(at, 2 * TILE), :]
        run_rows = run_w.T
        step_rows = step[pl.ds(at, 2 * TILE), :].T
        run_cols = run_w[TILE:, :]
        for pair in range(x_cols // 128):
            mixes = []
            for h in (2 * pair, 2 * pair + 1):
                gap = run_cols[:, h : h + 1] - run_rows[h : h + 1, :]
                mix = jnp.exp(jnp.where(mask, gap, -jnp.inf)) * score * step_rows[h : h + 1, :]
                mixes.append(mix.astype(BF16))
            here = slice(128 * pair, 128 * (pair + 1))
            x_w = xs[pl.ds(at, 2 * TILE), here]
            nothing = jnp.zeros_like(x_w)
            both = jnp.concatenate([jnp.where(left, x_w, nothing), jnp.where(left, nothing, x_w)], axis=0)
            out = dot(jnp.concatenate(mixes, axis=1), both)
            sum_ref[pair, pl.ds(at, TILE), :] = out + skip[:, here] * x_w[TILE:].astype(F32)
        return carry

    lax.fori_loop(0, rows // TILE, tile, 0, unroll=2)
    sum_ref[0 : x_cols // 128, rows:, :] = jnp.zeros((x_cols // 128, sum_ref.shape[1] - rows, 128), F32)
    fade_ref[rows:, :] = jnp.zeros((fade_ref.shape[0] - rows, 128), F32)
    add_carried(table, 0, parts, c_ref, fade_ref, states, sum_ref, state_sem)


def fetch_states(table, first, arrays, states, sems):
    state_size = states.shape[1]
    for k, array in enumerate(arrays):

        def begin(i, carry, array=array):
            at = pl.multiple_of(table[2, i] * state_size, state_size)
            pltpu.make_async_copy(array.at[pl.ds(at, state_size), :], states.at[i], sems.at[i]).start()
            return carry

        lax.fori_loop(table[3, first + k], table[3, first + k + 1], begin, 0)


def add_carried(table, first, arrays, c_ref, fade_ref, states, total, sems):
    requests, state_size, x_cols = states.shape
    begins, ends = table[3, first], table[3, first + len(arrays)]
    row = lax.broadcasted_iota(jnp.int32, (32, 128), 0)
    lane_head = lax.broadcasted_iota(jnp.int32, (128, x_cols), 1) // 64
    spread = jnp.where(lane_head == lax.broadcasted_iota(jnp.int32, (128, x_cols), 0), 1.0, 0.0).astype(BF16)
    side = 8

    def some(group, carry):
        picks = []
        for k in range(side):
            i = begins + group * side + k

            @pl.when(i < ends)
            def _():
                pltpu.make_async_copy(
                    arrays[0].at[pl.ds(0, state_size), :], states.at[i], sems.at[i]
                ).wait()

            safe = jnp.minimum(i, requests - 1)
            picks.append((safe, table[0, safe], jnp.where(i < ends, table[1, safe], 0)))
        terms = []
        for i, start, _ in picks:
            fade = fade_ref[pl.ds(start, 32), :]
            high = fade.astype(BF16)
            low = (fade - high.astype(F32)).astype(BF16)
            scale = dot(jnp.concatenate([high, low], axis=0), spread)
            product = dot(c_ref[pl.ds(start, 32), :].astype(BF16), states[i])
            terms.append((scale[0:32] + scale[32:64]) * product)
        for term, (_, start, length) in zip(terms, picks):
            inside = row < length
            for k in range(x_cols // 128):
                old = total[k, pl.ds(start, 32), :]
                total[k, pl.ds(start, 32), :] = jnp.where(
                    inside, old + term[:, 128 * k : 128 * (k + 1)], old
                )
        return carry

    lax.fori_loop(0, lax.div(ends - begins + side - 1, side), some, 0)


def late_kernel(first, count, table, *refs):
    arrays, (before, out, states, total, sems, got) = refs[:count], refs[count:]
    rows, x_cols = out.shape
    c_ref, fade_ref = total.at[x_cols // 128], total.at[x_cols // 128 + 1]
    copy = pltpu.make_async_copy(before, total, got)
    copy.start()
    fetch_states(table, first, arrays, states, sems)
    copy.wait()
    add_carried(table, first, arrays, c_ref, fade_ref, states, total, sems)
    for k in range(x_cols // 128):
        out[:, 128 * k : 128 * (k + 1)] = total[k, 0:rows, :].astype(BF16)


VMEM = pl.BlockSpec(memory_space=pltpu.VMEM)
SMEM = pl.BlockSpec(memory_space=pltpu.SMEM)
HBM = pl.BlockSpec(memory_space=pltpu.HBM)
ANY = pl.BlockSpec(memory_space=pl.ANY)


def weight_scratch(weights, rows, copies):
    depth, x_cols = weights[0].shape
    return [
        pltpu.VMEM((rows, depth), BF16),
        pltpu.VMEM((depth, x_cols), BF16),
        pltpu.VMEM((depth, weights[1].shape[1]), BF16),
        pltpu.VMEM((128, depth), BF16),
        pltpu.SemaphoreType.DMA((copies + 2 + x_cols // WIDE,)),
    ]


def project(blocks, weights, flops):
    rows, x_cols = sum(b.shape[0] for b in blocks), weights[0].shape[1]
    return pl.pallas_call(
        project_kernel,
        out_shape=(
            jax.ShapeDtypeStruct((rows, x_cols), BF16),
            jax.ShapeDtypeStruct((rows, weights[1].shape[1] + 128), BF16),
        ),
        in_specs=[HBM] * (len(blocks) + 3),
        out_specs=(VMEM, VMEM),
        scratch_shapes=weight_scratch(weights, rows, len(blocks)),
        compiler_params=pltpu.CompilerParams(vmem_limit_bytes=MOST),
        cost_estimate=pl.CostEstimate(flops=flops, bytes_accessed=14000000, transcendentals=0),
        name="project",
    )(*blocks, *weights)


def mixer_inner(z, table, parts, priors, projected, info, columns, taps, bias, decay, skip):
    rows = sum(p[0].shape[0] for p in projected)
    x_cols, cols = projected[0][0].shape[1], taps.shape[1]
    requests, state_size, margin = table.shape[1] - 1, 128, 32
    return pl.pallas_call(
        inner_kernel,
        out_shape=jax.ShapeDtypeStruct((x_cols // 128 + 2, rows + margin, 128), F32),
        in_specs=[SMEM] * 2 + [HBM] * 6 + [VMEM] * 10,
        out_specs=VMEM,
        scratch_shapes=[
            pltpu.VMEM((rows + 8, cols), F32),
            pltpu.VMEM((rows + TILE, x_cols), BF16),
            pltpu.VMEM((rows + TILE, 128), BF16),
            pltpu.VMEM((rows, 128), BF16),
            pltpu.VMEM((rows + TILE, 128), F32),
            pltpu.VMEM((rows + TILE, 128), F32),
            pltpu.VMEM((requests, state_size, x_cols), BF16),
            pltpu.SemaphoreType.DMA((requests,)),
            pltpu.VMEM((8 * PRIORS, x_cols), BF16),
            pltpu.SemaphoreType.DMA((2,)),
        ],
        compiler_params=pltpu.CompilerParams(vmem_limit_bytes=MOST),
        cost_estimate=pl.CostEstimate(flops=14000000000, bytes_accessed=18000000, transcendentals=2000000),
        name="mixer_inner",
    )(z, table, *parts, *priors, *projected[0], *projected[1], info, columns, taps, bias, decay, skip)


def mixer_late(table, first, arrays, total, rows):
    x_cols = (total.shape[0] - 2) * 128
    state_size, requests = total.shape[2], table.shape[1] - 1
    return pl.pallas_call(
        lambda *refs: late_kernel(first, len(arrays), *refs),
        out_shape=jax.ShapeDtypeStruct((rows, x_cols), BF16),
        in_specs=[SMEM] + [ANY] * (len(arrays) + 1),
        out_specs=VMEM,
        scratch_shapes=[
            pltpu.VMEM((requests, state_size, x_cols), BF16),
            pltpu.VMEM(total.shape, F32),
            pltpu.SemaphoreType.DMA((requests,)),
            pltpu.SemaphoreType.DMA,
        ],
        compiler_params=pltpu.CompilerParams(vmem_limit_bytes=24 * 1024 * 1024),
        cost_estimate=pl.CostEstimate(flops=500000000, bytes_accessed=13000000, transcendentals=0),
        name="mixer_late",
    )(table, *arrays, total)


def shards(
    tokens, weight_x, weight_bc, weight_dt, kernel_x, kernel_bc, dt_bias, decay_rate, skip_gain,
    ssm_pool, conv_x_pool, conv_bc_pool, hit_holder, hit_slot, suffix_len,
):
    model_dim, heads = weight_dt.shape
    x_cols = weight_x.shape[1]
    bc_cols = weight_bc.shape[1] * weight_bc.shape[2]
    slots, head_size, state_size = ssm_pool.shape[0], ssm_pool.shape[2], ssm_pool.shape[3]
    requests = suffix_len.shape[1]
    me, z = lax.axis_index("cache"), lax.axis_index("tp")

    weights = (weight_x, weight_bc.reshape(model_dim, bc_cols), weight_dt.T)

    lengths = suffix_len[0]
    order = jnp.arange(requests, dtype=jnp.int32)
    ends = jnp.sum(jnp.where(order[None, :] <= order[:, None], lengths[None, :], 0), axis=1)
    starts = ends - lengths
    holder = lax.dynamic_slice_in_dim(hit_holder[:, 0], me * requests, requests)
    slot = lax.dynamic_slice_in_dim(hit_slot, me * requests, requests)
    my_y, my_x, my_c = me // (2 * NX), (me // 2) % NX, me % 2
    at_y, at_x, at_c = holder // (2 * NX), (holder // 2) % NX, holder % 2
    far_y, far_x = (my_y - at_y) % NY, (my_x - at_x) % NX
    outer, inner = jnp.where(at_c == 0, far_y, far_x), jnp.where(at_c == 0, far_x, far_y)
    node = jnp.where(inner == 2, 3, jnp.where(inner == 3, 2, inner))
    line = jnp.where(outer == 2, 3, jnp.where(outer == 3, 2, outer))
    prior_row = ((at_c != my_c) * NY + line) * PRIORS + node * PRIOR + slot * 3
    block = 2 * node + slot
    part_of = jnp.where(outer == 2, 3 + block // 4, line)
    block = jnp.where(outer == 2, block % 4, block)
    own = at_c == my_c
    array = jnp.where(
        part_of < 3,
        jnp.where(part_of == 0, jnp.where(own, 0, 1), jnp.where(own, 1, 3) + part_of),
        jnp.where(own, 0, 1) + 2 * part_of,
    )
    key = array * requests + order
    rank = jnp.sum((key[None, :] < key[:, None]).astype(jnp.int32), axis=1)
    sorting = (rank[None, :] == order[:, None]).astype(jnp.int32)
    by_array = jnp.sum(sorting[None] * jnp.stack([starts, lengths, block])[:, None, :], axis=2)
    firsts = jnp.sum((array[None, :] < order[:, None]).astype(jnp.int32), axis=1)
    table = jnp.concatenate([by_array, firsts[None]], axis=0).astype(jnp.int32)
    table = jnp.pad(table, ((0, 0), (0, 1)))
    info = jnp.stack([ends, starts])
    info = jnp.concatenate([info, jnp.full((2, 128 - requests), 1 << 20, jnp.int32)], axis=1)

    taps = jnp.concatenate([kernel_x, kernel_bc.reshape(4, bc_cols)], axis=1).astype(F32)
    pad = (0, 128 - heads)
    from_row = (prior_row[:, None] + jnp.arange(3)[None, :]).reshape(-1)
    from_row = jnp.pad(from_row, (0, 128 - 3 * requests), constant_values=-16)
    columns = jnp.pad(jnp.stack([from_row, info[0]]).astype(F32), ((0, 6), (0, 0)))
    tables = (
        table, weights, info, columns, taps, jnp.pad(dt_bias, pad)[None], jnp.pad(decay_rate, pad)[None],
        jnp.repeat(skip_gain, head_size)[None],
    )

    def inner(projected, parts, priors, tables):
        table, _, info, columns, taps, bias, decay, skip = tables
        sums = mixer_inner(
            z.reshape(1), table, parts, priors, projected, info, columns, taps,
            bias, decay, skip,
        )
        return sums, table

    states = jnp.swapaxes(ssm_pool.reshape(slots, heads * head_size, state_size), 1, 2)
    conv_bc = jnp.pad(conv_bc_pool.reshape(slots * 3, bc_cols), ((0, PRIOR - 12), (0, x_cols - bc_cols)))
    pool = jnp.concatenate(
        [states.reshape(slots * state_size, x_cols), conv_x_pool.reshape(slots * 3, x_cols), conv_bc]
    )
    late, (total, table) = gather(pool, tokens, tables, project, inner)
    return mixer_late(table, 4, late, total, NZ * tokens.shape[0])


def solution(mesh):
    in_specs = (
        P(("cache", "tp"), None), P(None, "tp"), P(None, None, "tp"), P(None, "tp"), P(None, "tp"),
        P(None, None, "tp"), P("tp"), P("tp"), P("tp"), P("cache", "tp", None, None), P("cache", None, "tp"),
        P("cache", None, None, "tp"), P(), P(), P("cache", None),
    )
    return jax.shard_map(
        shards, mesh=mesh, in_specs=in_specs, out_specs=P("cache", "tp"), check_vma=False
    )
```
